32 devices in a mesh: opair: 8 (over z, core), vpair: 4 (over y, x).
Axes of the slice: x: 2, y: 2, z: 4, core: 2. Of those that a mesh axis runs over, the one named last changes fastest.
Arguments:
- amplitudes: bfloat16 [2048, 4096], P('opair', 'vpair'), may hold values from -6 to 6
- tile_live: int32 [16, 32], P('opair', 'vpair'), may hold values 0 or 1
- integrals: bfloat16 [32, 24, 128, 128], P('vpair', 'opair'), may hold values from -0.109375 to 0.109375
- integral_columns: int32 [32, 24], P('vpair', 'opair'), may hold values from 0 to 31, as said below
- driver_terms: bfloat16 [2048, 4096], P('opair', 'vpair'), may hold values from -6 to 6
- occupied_energy: float32 [2048], P('opair'), may hold values from -3 to -0.8
- virtual_energy: float32 [4096], P('vpair'), may hold values from 0.4 to 4
Outputs:
- new_amplitudes: bfloat16 [2048, 4096], P('opair', 'vpair')
- residual: float32 [2048, 4096], P('opair', 'vpair')
The draws below stay inside these ranges and needn't reach their ends.
Inputs may be any that keep to these rules, and one draw needn't show every extreme that they name: `integral_columns`: the 24 entries of one row are distinct. Of the 24 entries that one device holds, at most 6 name column tiles of one index d of vpair (tiles d * 8 to d * 8 + 7), and on every device some index of vpair is named exactly 6 times.
All inputs are finite; a program needn't handle non-finite values. No bound on the sum of `tile_live` on one device may be relied on, other than what follows from the above.
Results may differ from the reference program's by a relative error of at most 0.015.
Values may be sent and summed in bfloat16 or wider, within the bound.
No kernel may reach another device: no remote copies, remote signals or barrier semaphores. Data moves between devices by JAX's collectives and lax.ppermute only.
A program may use at most 128 MiB of HBM per device.

```python
import jax
import jax.numpy as jnp
from jax import lax

TILE = 128
VTILE_DEV = 8
SLOT_DEV = 3
OTILES = 16
VTILES = 32
SLOTS = 24
OPAIRS = 2048
VPAIRS = 4096


def draw_integral_columns(key, part):
    key = jax.random.fold_in(key, 11)
    dest_key, order_key = jax.random.split(key)
    peer_total = VTILES // VTILE_DEV
    dest_perms = jax.vmap(lambda one_key: jax.random.permutation(one_key, peer_total))(jax.random.split(dest_key, peer_total))
    order_perms = jax.vmap(lambda one_key: jax.random.permutation(one_key, VTILE_DEV))(jax.random.split(order_key, VTILES * peer_total)).reshape(VTILES, peer_total, VTILE_DEV)
    row_tiles = jnp.arange(VTILES, dtype=jnp.int32)[:, None]
    slot_ids = jnp.arange(SLOTS, dtype=jnp.int32)[None, :]
    spread = row_tiles % VTILE_DEV * SLOT_DEV + slot_ids
    residue = spread % peer_total
    layer_index = spread // peer_total % VTILE_DEV
    owner_dev = dest_perms[row_tiles // VTILE_DEV, residue].astype(jnp.int32)
    within_dev = order_perms[row_tiles, owner_dev, layer_index].astype(jnp.int32)
    return (owner_dev * VTILE_DEV + within_dev).astype(jnp.int32)


def touch_ends(values, own_key, least, largest):
    spot = [jax.random.randint(jax.random.fold_in(own_key, axis), (), 0, length) for axis, length in enumerate(values.shape)]
    longest = values.shape.index(max(values.shape))
    neighbour = spot[:longest] + [(spot[longest] + 1) % values.shape[longest]] + spot[longest + 1:]
    return values.at[tuple(spot)].set(least).at[tuple(neighbour)].set(largest)


def levels(rng, extent, cuts, smallest, largest):
    def one(axis_at, blocks):
        steps = jax.random.uniform(jax.random.fold_in(jax.random.fold_in(rng, 6), axis_at), (blocks,), jnp.float32, smallest / len(cuts), largest / len(cuts))
        return jnp.repeat(jnp.exp(steps), extent[axis_at] // blocks).reshape((-1,) + (1,) * (len(extent) - axis_at - 1))

    level = one(*cuts[0])
    for cut in cuts[1:]:
        level = level * one(*cut)
    return level


def scatter_about(key, shape, scale, most, cuts=(), kind=jnp.bfloat16):
    factor_of = levels(key, shape, cuts, -0.22, 0.18) if cuts else 1.0
    drawn = jax.random.normal(key, shape, jnp.float32) * scale * factor_of
    return jnp.minimum(jnp.maximum(drawn, -most), most).astype(kind)


def setup_inputs(seed: int = 0) -> dict:
    key_list = jax.random.split(jax.random.key(seed), 8)
    amplitudes = scatter_about(key_list[0], (OPAIRS, VPAIRS), 1.0, 6.0, ((0, 8), (1, 4)))
    tile_live = touch_ends((jax.random.randint(key_list[1], (OTILES, VTILES), 0, 4) < 3).astype(jnp.int32), jax.random.fold_in(key_list[1], 1), 0, 1)
    integrals = scatter_about(key_list[2], (VTILES, SLOTS, TILE, TILE), (SLOTS * TILE) ** -0.5, 0.109375, ((0, 4), (1, 8)))
    integral_columns = draw_integral_columns(jax.random.fold_in(key_list[7], 71), 0)
    driver_terms = scatter_about(key_list[4], (OPAIRS, VPAIRS), 1.0, 6.0, ((0, 8), (1, 4)))
    occupied_energy = jnp.clip(-3.0 + 2.2 * jax.random.uniform(key_list[5], (OPAIRS,), jnp.float32) ** levels(key_list[5], (OPAIRS,), ((0, 8),), -0.2, 0.2), -3.0, -0.8)
    virtual_energy = jnp.clip(0.4 + 3.6 * jax.random.uniform(key_list[6], (VPAIRS,), jnp.float32) ** levels(key_list[6], (VPAIRS,), ((0, 4),), -0.2, 0.2), 0.4, 4.0)
    return dict(amplitudes=amplitudes, tile_live=tile_live, integrals=integrals, integral_columns=integral_columns, driver_terms=driver_terms, occupied_energy=occupied_energy, virtual_energy=virtual_energy)


def reference(amplitudes, tile_live, integrals, integral_columns, driver_terms, occupied_energy, virtual_energy):
    live_mask = jnp.broadcast_to(tile_live[:, None, :, None].astype(jnp.float32), (OTILES, TILE, VTILES, TILE)).reshape(OPAIRS, VPAIRS)
    masked = (amplitudes.astype(jnp.float32) * live_mask).astype(jnp.bfloat16)

    def accumulate(ladder_sum, row_tile):
        panel_cols = lax.dynamic_slice_in_dim(masked, row_tile * TILE, TILE, 1).astype(jnp.float32)
        tile_block = lax.dynamic_index_in_dim(integrals, row_tile, 0, keepdims=False).astype(jnp.float32)
        products = jnp.einsum("rx,kxy->rky", panel_cols, tile_block, precision=lax.Precision.HIGHEST)
        targets = lax.dynamic_index_in_dim(integral_columns, row_tile, 0, keepdims=False)
        return ladder_sum.at[:, targets, :].add(products), jnp.zeros((), jnp.float32)

    result = lax.scan(accumulate, jnp.zeros((OPAIRS, VTILES, TILE), jnp.float32), jnp.arange(VTILES, dtype=jnp.int32))
    ladder = result[0].reshape(OPAIRS, VPAIRS)
    denominator = occupied_energy[:, None] - virtual_energy[None, :]
    residual = (driver_terms.astype(jnp.float32) + ladder + denominator * amplitudes.astype(jnp.float32)) * live_mask
    new_amplitudes = (masked.astype(jnp.float32) - residual / denominator).astype(jnp.bfloat16)
    return new_amplitudes, residual
```

```python
import functools

import jax
import jax.numpy as jnp
from jax import lax
from jax.experimental import pallas as pl
from jax.experimental.pallas import tpu as pltpu
from jax.sharding import PartitionSpec as P

VMEM_BYTES = 56 * 1024 * 1024
CORES = 2


def pack_kernel(n_v, columns, live, integrals, amplitudes, *refs):
    packed, masked, counts, sems = refs[:n_v], refs[n_v], refs[n_v + 1], refs[n_v + 2]
    rows, slots, tile, _ = integrals.shape
    me = lax.axis_index("vpair")
    for j in range(n_v):
        counts[j] = 0

    def send(entry, carry):
        row, slot = lax.div(entry, slots), lax.rem(entry, slots)
        partner = lax.div(columns[entry], rows) ^ me
        place = counts[partner]
        counts[partner] = place + 1
        for j in range(n_v):

            @pl.when(partner == j)
            def _():
                pltpu.make_async_copy(
                    integrals.at[row, slot], packed[j].at[place], sems.at[entry]
                ).start()

        return carry

    lax.fori_loop(0, rows * slots, send, 0)
    for o in range(live.shape[0]):
        for c in range(live.shape[1]):
            at = (pl.ds(o * tile, tile), pl.ds(c * tile, tile))
            kept = live[o, c].astype(jnp.float32)
            masked[at] = (amplitudes[at].astype(jnp.float32) * kept).astype(masked.dtype)

    def finish(entry, carry):
        pltpu.make_async_copy(integrals.at[0, 0], packed[0].at[0], sems.at[entry]).wait()
        return carry

    lax.fori_loop(0, rows * slots, finish, 0)


def ladder_kernel(n_v, n_z, n_groups, cap, table, *refs):
    n_steps = 2 * n_z - 1
    n_shards = n_groups * n_steps
    group = n_v // n_groups
    own_a, refs = refs[:n_v], refs[n_v:]
    twin_a, refs = refs[:n_v], refs[n_v:]
    shards, refs = refs[:n_shards], refs[n_shards:]
    own_out, twin_out, a_buf, tile_buf, total, a_sems, tile_sems = refs
    n_rows, _ = own_a[0].shape
    tile = tile_buf.shape[-1]
    col_tiles = own_out.shape[0]
    v = lax.axis_index("vpair")
    o = lax.axis_index("opair")
    z, core = lax.div(o, CORES), lax.rem(o, CORES)

    def source_z(step):
        return jnp.where(step < n_z, z - step, z + step - n_z + 1)

    def valid(step):
        return (source_z(step) >= 0) & (source_z(step) < n_z)

    a_copies = []
    for j in range(n_v):
        for half, ref in ((0, own_a[j]), (1, twin_a[j])):
            copy = pltpu.make_async_copy(
                ref, a_buf.at[j, pl.ds(half * n_rows, n_rows)], a_sems.at[2 * j + half]
            )
            copy.start()
            a_copies.append(copy)
    for i in range(n_shards):

        @pl.when(valid(i % n_steps))
        def _(i=i):
            pltpu.make_async_copy(shards[i], tile_buf.at[i], tile_sems.at[i]).start()

    total[...] = jnp.zeros_like(total)
    for copy in a_copies:
        copy.wait()

    def one_shard(i, carry):
        step = lax.rem(i, n_steps)

        @pl.when(valid(step))
        def _():
            pltpu.make_async_copy(shards[0], tile_buf.at[i], tile_sems.at[i]).wait()
            for member in range(group):
                j = lax.div(i, n_steps) * group + member
                device = (source_z(step) * CORES + core) * n_v + (v ^ j)

                def one_entry(entry, place):
                    column = table[device, entry]
                    hit = lax.div(column, col_tiles) == v

                    @pl.when(hit)
                    def _():
                        row = lax.div(entry, table.shape[1] // col_tiles)
                        left = a_buf[j, :, pl.ds(pl.multiple_of(row * tile, tile), tile)]
                        total[lax.rem(column, col_tiles)] += jnp.dot(
                            left,
                            tile_buf[i, member * cap + place],
                            preferred_element_type=jnp.float32,
                        )

                    return place + hit.astype(jnp.int32)

                lax.fori_loop(0, table.shape[1], one_entry, 0)

        return carry

    lax.fori_loop(0, n_shards, one_shard, 0)
    own_out[...] = total[:, :n_rows]
    twin_out[...] = total[:, n_rows:].astype(twin_out.dtype)


def update_kernel(live, amplitudes, driver, own, twin, occupied, virtual, new, residual):
    tile = own.shape[-1]
    for o in range(live.shape[0]):
        for c in range(live.shape[1]):
            rows = pl.ds(o * tile, tile)
            at = (rows, pl.ds(c * tile, tile))
            kept = live[o, c].astype(jnp.float32)
            amps = amplitudes[at].astype(jnp.float32)
            masked = (amps * kept).astype(jnp.bfloat16).astype(jnp.float32)
            ladder = own[c, rows] + twin[c, rows].astype(jnp.float32)
            denominator = occupied[rows, :] - virtual[:, pl.ds(c * tile, tile)]
            rest = (driver[at].astype(jnp.float32) + ladder + denominator * amps) * kept
            residual[at] = rest
            new[at] = (masked - rest / denominator).astype(new.dtype)


def on_device(
    amplitudes,
    tile_live,
    integrals,
    integral_columns,
    driver_terms,
    occupied_energy,
    virtual_energy,
):
    n_rows, width = amplitudes.shape
    row_tiles, slots, tile, _ = integrals.shape
    n_v, n_o = lax.axis_size("vpair"), lax.axis_size("opair")
    n_z = n_o // CORES
    entries = row_tiles * slots
    cap = -(-entries // n_v)
    n_groups = min(n_v, 4)
    group = n_v // n_groups
    in_smem = pl.BlockSpec(memory_space=pltpu.SMEM)
    in_vmem = pl.BlockSpec(memory_space=pltpu.VMEM)
    anywhere = pl.BlockSpec(memory_space=pl.ANY)
    flat_columns = integral_columns.reshape(entries)

    *packed, masked = pl.pallas_call(
        functools.partial(pack_kernel, n_v),
        out_shape=[jax.ShapeDtypeStruct((cap, tile, tile), integrals.dtype)] * n_v
        + [jax.ShapeDtypeStruct(amplitudes.shape, amplitudes.dtype)],
        in_specs=[in_smem, in_smem, anywhere, in_vmem],
        out_specs=[anywhere] * n_v + [in_vmem],
        scratch_shapes=[pltpu.SMEM((n_v,), jnp.int32), pltpu.SemaphoreType.DMA((entries,))],
        compiler_params=pltpu.CompilerParams(vmem_limit_bytes=VMEM_BYTES),
        name="pack",
    )(flat_columns, tile_live, integrals, amplitudes)

    table = lax.all_gather(flat_columns, ("opair", "vpair"))

    def across_v(value, j):
        return lax.ppermute(value, "vpair", [(i, i ^ j) for i in range(n_v)]) if j else value

    def across_core(value):
        return lax.ppermute(value, "opair", [(i, i ^ 1) for i in range(n_o)])

    def along_z(value, hop):
        pairs = [(i, i + hop * CORES) for i in range(n_o) if 0 <= i + hop * CORES < n_o]
        return lax.ppermute(value, "opair", pairs)

    chunks = [across_v(packed[j], j) for j in range(n_v)]
    shards = []
    for g in range(n_groups):
        members = chunks[g * group : (g + 1) * group]
        start = members[0] if group == 1 else jnp.concatenate(members)
        shards.append(start)
        for hop in (1, -1):
            moving = start
            for _ in range(n_z - 1):
                moving = along_z(moving, hop)
                shards.append(moving)
    own_a = [across_v(masked, j) for j in range(n_v)]
    twin_a = [across_core(value) for value in own_a]

    own, twin = pl.pallas_call(
        functools.partial(ladder_kernel, n_v, n_z, n_groups, cap),
        out_shape=[
            jax.ShapeDtypeStruct((row_tiles, n_rows, tile), jnp.float32),
            jax.ShapeDtypeStruct((row_tiles, n_rows, tile), jnp.bfloat16),
        ],
        in_specs=[in_smem] + [anywhere] * (2 * n_v + len(shards)),
        out_specs=[in_vmem, in_vmem],
        scratch_shapes=[
            pltpu.VMEM((n_v, CORES * n_rows, width), amplitudes.dtype),
            pltpu.VMEM((len(shards), group * cap, tile, tile), integrals.dtype),
            pltpu.VMEM((row_tiles, CORES * n_rows, tile), jnp.float32),
            pltpu.SemaphoreType.DMA((2 * n_v,)),
            pltpu.SemaphoreType.DMA((len(shards),)),
        ],
        compiler_params=pltpu.CompilerParams(vmem_limit_bytes=VMEM_BYTES),
        name="ladder",
    )(table, *own_a, *twin_a, *shards)
    twin = across_core(twin)

    return pl.pallas_call(
        update_kernel,
        out_shape=[
            jax.ShapeDtypeStruct((n_rows, width), jnp.bfloat16),
            jax.ShapeDtypeStruct((n_rows, width), jnp.float32),
        ],
        in_specs=[in_smem] + [in_vmem] * 6,
        out_specs=[in_vmem, in_vmem],
        compiler_params=pltpu.CompilerParams(vmem_limit_bytes=VMEM_BYTES),
        name="update",
    )(
        tile_live,
        amplitudes,
        driver_terms,
        own,
        twin,
        jnp.broadcast_to(occupied_energy[:, None], (n_rows, tile)),
        virtual_energy.reshape(1, width),
    )


def solution(mesh):
    in_specs = (
        P("opair", "vpair"),
        P("opair", "vpair"),
        P("vpair", "opair", None, None),
        P("vpair", "opair"),
        P("opair", "vpair"),
        P("opair"),
        P("vpair"),
    )
    out_specs = (P("opair", "vpair"), P("opair", "vpair"))
    return jax.shard_map(
        on_device, mesh=mesh, in_specs=in_specs, out_specs=out_specs, check_vma=False
    )
```

```python
import functools

import jax
import jax.numpy as jnp
from jax import lax
from jax.experimental import pallas as pl
from jax.experimental.pallas import tpu as pltpu
from jax.sharding import PartitionSpec as P

VMEM_BYTES = 56 * 1024 * 1024
CORES = 2
NOTE_ROWS = 16


def pack_kernel(n_v, cap, columns, live, integrals, amplitudes, *refs):
    parcels, masked, origin, codes = refs[:n_v], refs[n_v], refs[n_v + 1], refs[n_v + 2]
    rows, slots, tile, _ = integrals.shape
    me = lax.axis_index("vpair")
    counts = [jnp.int32(0)] * n_v
    for i in range(n_v * cap):
        origin[i] = 0
        codes[i] = -1
    for row in range(rows):
        for slot in range(slots):
            column = columns[slot, row]
            partner = lax.div(column, rows) ^ me
            place = counts[0]
            for j in range(1, n_v):
                place = jnp.where(partner == j, counts[j], place)
            counts = [counts[j] + (partner == j).astype(jnp.int32) for j in range(n_v)]
            at = partner * cap + place
            origin[at] = row * slots + slot
            codes[at] = row * rows + lax.rem(column, rows)
    lane = lax.broadcasted_iota(jnp.int32, (NOTE_ROWS, tile), 1)
    for j in range(n_v):
        note = jnp.full((NOTE_ROWS, tile), -1, jnp.int32)
        for k in range(cap):
            entry = origin[j * cap + k]
            parcels[j][0, pl.ds(k * tile, tile)] = integrals[
                lax.div(entry, slots), lax.rem(entry, slots)
            ]
            note = jnp.where(lane == k, codes[j * cap + k], note)
        parcels[j][0, pl.ds(cap * tile, NOTE_ROWS)] = note.astype(jnp.float32).astype(
            integrals.dtype
        )
    for o in range(live.shape[0]):
        for c in range(live.shape[1]):
            at = (pl.ds(o * tile, tile), pl.ds(c * tile, tile))
            kept = live[o, c].astype(jnp.float32)
            masked[at] = (amplitudes[at].astype(jnp.float32) * kept).astype(masked.dtype)


def read_notes(units, n_units, cap, rows, notes_wide, notes, sem):
    tile = units.shape[-1]
    for u in range(n_units):
        note = units[u, pl.ds(cap * tile, NOTE_ROWS)].astype(jnp.float32).astype(jnp.int32)
        notes_wide[pl.ds(u, 1)] = note[:1]
    copy = pltpu.make_async_copy(notes_wide, notes, sem)
    copy.start()
    copy.wait()


def add_unit(unit, j, cap, rows, amps, units, notes, total):
    tile = units.shape[-1]
    for k in range(cap):
        code = notes[unit, k]
        used = code >= 0
        row = jnp.where(used, lax.div(code, rows), 0)
        column = jnp.where(used, lax.rem(code, rows), rows)
        total[column] += jnp.dot(
            amps[j, :, pl.ds(pl.multiple_of(row * tile, tile), tile)],
            units[unit, pl.ds(k * tile, tile)],
            preferred_element_type=jnp.float32,
        )


def ladder_kernel(n_v, n_z, cap, rows, layout, occupied, *refs):
    own_a, refs = refs[:n_v], refs[n_v:]
    twin_a, refs = refs[:n_v], refs[n_v:]
    arrays, refs = refs[: len(layout)], refs[len(layout) :]
    own_out, twin_out, occupied_out = refs[:3]
    a_buf, units, notes_wide, notes, queue, total, a_sems, sems, note_sem = refs[3:]
    n_rows, _ = own_a[0].shape
    tile = units.shape[-1]
    z = lax.div(lax.axis_index("opair"), CORES)
    even = lax.rem(z, 2) == 0

    def valid(kind, hop):
        if kind == "own":
            return z >= 0
        upward = ~even if kind == "even" else even
        source = jnp.where(upward, z - 1 - hop, z + 1 + hop)
        return (source >= 0) & (source < n_z)

    a_copies = []
    for j in range(n_v):
        for half, ref in ((0, own_a[j]), (1, twin_a[j])):
            copy = pltpu.make_async_copy(
                ref, a_buf.at[j, pl.ds(half * n_rows, n_rows)], a_sems.at[2 * j + half]
            )
            copy.start()
            a_copies.append(copy)
    copies, first = [], 0
    for i, (kind, hop, partners) in enumerate(layout):
        copy = pltpu.make_async_copy(
            arrays[i], units.at[pl.ds(first, len(partners))], sems.at[i]
        )
        copy.start()
        copies.append(copy)
        first += len(partners)

    count, unit = jnp.int32(0), 0
    for kind, hop, partners in layout:
        use = valid(kind, hop).astype(jnp.int32)
        for j in partners:
            queue[0, count] = unit
            queue[1, count] = j
            count += use
            unit += 1
    total[...] = jnp.zeros_like(total)
    for o in range(n_rows // tile):
        wide = jnp.broadcast_to(occupied[pl.ds(o, 1)], (tile, tile))
        occupied_out[pl.ds(o * tile, tile)] = wide.T
    for copy in copies:
        copy.wait()
    read_notes(units, first, cap, rows, notes_wide, notes, note_sem)
    for copy in a_copies:
        copy.wait()

    def one(i, carry):
        add_unit(queue[0, i], queue[1, i], cap, rows, a_buf, units, notes, total)
        return carry

    lax.fori_loop(0, count, one, 0)
    own_out[...] = total[:rows, :n_rows]
    twin_out[...] = total[:rows, n_rows:].astype(twin_out.dtype)


def update_kernel(
    n_v, n_z, cap, partners, live, amplitudes, driver, own, twin, occupied, virtual, *refs
):
    a_own, refs = refs[:n_v], refs[n_v:]
    arrays, (new, residual, a_buf, units, notes_wide, notes, total, a_sems, sems, note_sem) = (
        refs[:CORES],
        refs[CORES:],
    )
    rows, _, tile = own.shape
    z = lax.div(lax.axis_index("opair"), CORES)
    total[pl.ds(0, rows)] = own[...] + twin[...].astype(jnp.float32)

    @pl.when((z == 0) | (z == n_z - 1))
    def _():
        a_copies = [
            pltpu.make_async_copy(a_own[j], a_buf.at[j], a_sems.at[j]) for j in range(n_v)
        ]
        copies = [
            pltpu.make_async_copy(
                arrays[i], units.at[pl.ds(i * len(partners), len(partners))], sems.at[i]
            )
            for i in range(CORES)
        ]
        for copy in copies + a_copies:
            copy.start()
        total[rows] = jnp.zeros_like(total[rows])
        for copy in copies:
            copy.wait()
        n_units = CORES * len(partners)
        read_notes(units, n_units, cap, rows, notes_wide, notes, note_sem)
        for copy in a_copies:
            copy.wait()

        def one(i, carry):
            j = lax.rem(i, len(partners)) + partners[0]
            add_unit(i, j, cap, rows, a_buf, units, notes, total)
            return carry

        lax.fori_loop(0, n_units, one, 0)

    for o in range(live.shape[0]):
        for c in range(live.shape[1]):
            here = pl.ds(o * tile, tile)
            at = (here, pl.ds(c * tile, tile))
            kept = live[o, c].astype(jnp.float32)
            amps = amplitudes[at].astype(jnp.float32)
            masked = (amps * kept).astype(jnp.bfloat16).astype(jnp.float32)
            denominator = occupied[here, :] - virtual[:, pl.ds(c * tile, tile)]
            rest = (
                driver[at].astype(jnp.float32) + total[c, here] + denominator * amps
            ) * kept
            residual[at] = rest
            new[at] = (masked - rest / denominator).astype(new.dtype)


def on_device(
    amplitudes,
    tile_live,
    integrals,
    integral_columns,
    driver_terms,
    occupied_energy,
    virtual_energy,
):
    n_rows, width = amplitudes.shape
    rows, slots, tile, _ = integrals.shape
    n_v, n_o = lax.axis_size("vpair"), lax.axis_size("opair")
    n_z = n_o // CORES
    cap = -(-(rows * slots) // n_v)
    height = cap * tile + NOTE_ROWS
    dtype = integrals.dtype
    in_smem = pl.BlockSpec(memory_space=pltpu.SMEM)
    in_vmem = pl.BlockSpec(memory_space=pltpu.VMEM)
    anywhere = pl.BlockSpec(memory_space=pl.ANY)
    params = pltpu.CompilerParams(vmem_limit_bytes=VMEM_BYTES)

    *parcels, masked = pl.pallas_call(
        functools.partial(pack_kernel, n_v, cap),
        out_shape=[jax.ShapeDtypeStruct((1, height, tile), dtype)] * n_v
        + [jax.ShapeDtypeStruct(amplitudes.shape, amplitudes.dtype)],
        in_specs=[in_smem, in_smem, in_vmem, in_vmem],
        out_specs=[in_vmem] * (n_v + 1),
        scratch_shapes=[pltpu.SMEM((n_v * cap,), jnp.int32)] * 2,
        compiler_params=params,
        name="pack",
    )(integral_columns.T, tile_live, integrals, amplitudes)

    def across_v(value, j):
        return lax.ppermute(value, "vpair", [(i, i ^ j) for i in range(n_v)]) if j else value

    def across_core(value):
        return lax.ppermute(value, "opair", [(i, i ^ 1) for i in range(n_o)])

    def swap_z(value, odd):
        pairs = []
        for z in range(n_z):
            partner = ((z + odd) ^ 1) - odd
            for core in range(CORES):
                target = (partner, core) if 0 <= partner < n_z else (z, core ^ 1)
                pairs.append((z * CORES + core, target[0] * CORES + target[1]))
        return lax.ppermute(value, "opair", pairs)

    def along_z(start):
        even, odd = [swap_z(start, 0)], [swap_z(start, 1)]
        for hop in range(1, n_z - 1):
            even.append(swap_z(odd[hop - 1], 0))
            if hop < n_z - 2:
                odd.append(swap_z(even[hop - 1], 1))
        return even, odd

    others = list(range(1, n_v))
    near = parcels[0]
    far = jnp.concatenate([across_v(parcels[j], j) for j in others])
    arrays, layout = [], []
    last = None
    for start, partners in ((near, [0]), (far, others)):
        even, odd = along_z(start)
        if start is far:
            last = even.pop()
        arrays += [start, *even, *odd]
        layout += [("own", 0, partners)]
        layout += [("even", hop, partners) for hop in range(len(even))]
        layout += [("odd", hop, partners) for hop in range(len(odd))]
    own_a = [across_v(masked, j) for j in range(n_v)]
    twin_a = [across_core(value) for value in own_a]
    n_units = sum(len(partners) for _, _, partners in layout)

    own, twin, occupied = pl.pallas_call(
        functools.partial(ladder_kernel, n_v, n_z, cap, rows, layout),
        out_shape=[
            jax.ShapeDtypeStruct((rows, n_rows, tile), jnp.float32),
            jax.ShapeDtypeStruct((rows, n_rows, tile), jnp.bfloat16),
            jax.ShapeDtypeStruct((n_rows, tile), jnp.float32),
        ],
        in_specs=[in_vmem] + [anywhere] * (2 * n_v + len(arrays)),
        out_specs=[in_vmem] * 3,
        scratch_shapes=[
            pltpu.VMEM((n_v, CORES * n_rows, width), amplitudes.dtype),
            pltpu.VMEM((n_units, height, tile), dtype),
            pltpu.VMEM((n_units, tile), jnp.int32),
            pltpu.SMEM((n_units, tile), jnp.int32),
            pltpu.SMEM((2, n_units + 1), jnp.int32),
            pltpu.VMEM((rows + 1, CORES * n_rows, tile), jnp.float32),
            pltpu.SemaphoreType.DMA((2 * n_v,)),
            pltpu.SemaphoreType.DMA((len(arrays),)),
            pltpu.SemaphoreType.DMA,
        ],
        compiler_params=params,
        cost_estimate=pl.CostEstimate(
            flops=8 * n_units * cap * n_rows * tile * tile * CORES,
            bytes_accessed=16 * 1024 * 1024,
            transcendentals=0,
        ),
        name="ladder",
    )(occupied_energy.reshape(-1, tile), *own_a, *twin_a, *arrays)
    twin = across_core(twin)
    n_last = CORES * len(others)

    return pl.pallas_call(
        functools.partial(update_kernel, n_v, n_z, cap, others),
        out_shape=[
            jax.ShapeDtypeStruct((n_rows, width), jnp.bfloat16),
            jax.ShapeDtypeStruct((n_rows, width), jnp.float32),
        ],
        in_specs=[in_smem] + [in_vmem] * 6 + [anywhere] * (n_v + CORES),
        out_specs=[in_vmem] * 2,
        scratch_shapes=[
            pltpu.VMEM((n_v, n_rows, width), amplitudes.dtype),
            pltpu.VMEM((n_last, height, tile), dtype),
            pltpu.VMEM((n_last, tile), jnp.int32),
            pltpu.SMEM((n_last, tile), jnp.int32),
            pltpu.VMEM((rows + 1, n_rows, tile), jnp.float32),
            pltpu.SemaphoreType.DMA((n_v,)),
            pltpu.SemaphoreType.DMA((CORES,)),
            pltpu.SemaphoreType.DMA,
        ],
        compiler_params=params,
        name="update",
    )(
        tile_live,
        amplitudes,
        driver_terms,
        own,
        twin,
        occupied,
        virtual_energy.reshape(1, width),
        *own_a,
        last,
        across_core(last),
    )


def solution(mesh):
    in_specs = (
        P("opair", "vpair"),
        P("opair", "vpair"),
        P("vpair", "opair", None, None),
        P("vpair", "opair"),
        P("opair", "vpair"),
        P("opair"),
        P("vpair"),
    )
    out_specs = (P("opair", "vpair"), P("opair", "vpair"))
    return jax.shard_map(
        on_device, mesh=mesh, in_specs=in_specs, out_specs=out_specs, check_vma=False
    )
```

```python
import functools

import jax
import jax.numpy as jnp
from jax import lax
from jax.experimental import pallas as pl
from jax.experimental.pallas import tpu as pltpu
from jax.sharding import PartitionSpec as P

VMEM_BYTES = 56 * 1024 * 1024
CORES = 2
NOTE_ROWS = 16


def pack_kernel(n_v, cap, columns, live, integrals, amplitudes, *refs):
    parcels, masked, origin, codes = refs[:n_v], refs[n_v], refs[n_v + 1], refs[n_v + 2]
    rows, slots, tile, _ = integrals.shape
    me = lax.axis_index("vpair")
    counts = [jnp.int32(0)] * n_v
    for i in range(n_v * cap):
        origin[i] = 0
        codes[i] = -1
    for row in range(rows):
        for slot in range(slots):
            column = columns[slot, row]
            partner = lax.div(column, rows) ^ me
            place = counts[0]
            for j in range(1, n_v):
                place = jnp.where(partner == j, counts[j], place)
            counts = [counts[j] + (partner == j).astype(jnp.int32) for j in range(n_v)]
            at = partner * cap + place
            origin[at] = row * slots + slot
            codes[at] = row * rows + lax.rem(column, rows)
    lane = lax.broadcasted_iota(jnp.int32, (NOTE_ROWS, tile), 1)
    for j in range(n_v):
        note = jnp.full((NOTE_ROWS, tile), -1, jnp.int32)
        for k in range(cap):
            entry = origin[j * cap + k]
            parcels[j][0, pl.ds(k * tile, tile)] = integrals[
                lax.div(entry, slots), lax.rem(entry, slots)
            ]
            note = jnp.where(lane == k, codes[j * cap + k], note)
        parcels[j][0, pl.ds(cap * tile, NOTE_ROWS)] = note.astype(jnp.float32).astype(
            integrals.dtype
        )
    for o in range(live.shape[0]):
        for c in range(live.shape[1]):
            at = (pl.ds(o * tile, tile), pl.ds(c * tile, tile))
            kept = live[o, c].astype(jnp.float32)
            masked[at] = (amplitudes[at].astype(jnp.float32) * kept).astype(masked.dtype)


def read_notes(units, n_units, cap, rows, notes_wide, notes, sem):
    tile = units.shape[-1]
    for u in range(n_units):
        note = units[u, pl.ds(cap * tile, NOTE_ROWS)].astype(jnp.float32).astype(jnp.int32)
        notes_wide[pl.ds(u, 1)] = note[:1]
    copy = pltpu.make_async_copy(notes_wide, notes, sem)
    copy.start()
    copy.wait()


def add_unit(unit, j, cap, rows, amps, units, notes, total):
    tile = units.shape[-1]
    for k in range(cap):
        code = notes[unit, k]
        used = code >= 0
        row = jnp.where(used, lax.div(code, rows), 0)
        column = jnp.where(used, lax.rem(code, rows), rows)
        total[column] += jnp.dot(
            amps[j, :, pl.ds(pl.multiple_of(row * tile, tile), tile)],
            units[unit, pl.ds(k * tile, tile)],
            preferred_element_type=jnp.float32,
        )


def ladder_kernel(n_v, n_z, cap, rows, layout, occupied, *refs):
    own_a, refs = refs[:n_v], refs[n_v:]
    twin_a, refs = refs[:n_v], refs[n_v:]
    arrays, refs = refs[: len(layout)], refs[len(layout) :]
    own_out, twin_out, occupied_out = refs[:3]
    a_buf, units, notes_wide, notes, queue, total, a_sems, sems, note_sem = refs[3:]
    n_rows, _ = own_a[0].shape
    tile = units.shape[-1]
    z = lax.div(lax.axis_index("opair"), CORES)
    even = lax.rem(z, 2) == 0

    def valid(kind, hop):
        if kind == "own":
            return z >= 0
        upward = ~even if kind == "even" else even
        source = jnp.where(upward, z - 1 - hop, z + 1 + hop)
        return (source >= 0) & (source < n_z)

    a_copies = []
    for j in range(n_v):
        for half, ref in ((0, own_a[j]), (1, twin_a[j])):
            copy = pltpu.make_async_copy(
                ref, a_buf.at[j, pl.ds(half * n_rows, n_rows)], a_sems.at[2 * j + half]
            )
            copy.start()
            a_copies.append(copy)
    copies, first = [], 0
    for i, (kind, hop, partners) in enumerate(layout):
        copy = pltpu.make_async_copy(
            arrays[i], units.at[pl.ds(first, len(partners))], sems.at[i]
        )
        copy.start()
        copies.append(copy)
        first += len(partners)

    count, unit = jnp.int32(0), 0
    for kind, hop, partners in layout:
        use = valid(kind, hop).astype(jnp.int32)
        for j in partners:
            queue[0, count] = unit
            queue[1, count] = j
            count += use
            unit += 1
    total[...] = jnp.zeros_like(total)
    for o in range(n_rows // tile):
        wide = jnp.broadcast_to(occupied[pl.ds(o, 1)], (tile, tile))
        occupied_out[pl.ds(o * tile, tile)] = wide.T
    for copy in copies:
        copy.wait()
    read_notes(units, first, cap, rows, notes_wide, notes, note_sem)
    for copy in a_copies:
        copy.wait()

    def one(i, carry):
        add_unit(queue[0, i], queue[1, i], cap, rows, a_buf, units, notes, total)
        return carry

    lax.fori_loop(0, count, one, 0)
    own_out[...] = total[:rows, :n_rows]
    twin_out[...] = total[:rows, n_rows:].astype(twin_out.dtype)


def update_kernel(
    n_v, n_z, cap, partners, live, amplitudes, driver, own, twin, occupied, virtual, *refs
):
    a_own, refs = refs[:n_v], refs[n_v:]
    arrays, (new, residual, a_buf, units, notes_wide, notes, total, a_sems, sems, note_sem) = (
        refs[:CORES],
        refs[CORES:],
    )
    rows, _, tile = own.shape
    z = lax.div(lax.axis_index("opair"), CORES)
    total[pl.ds(0, rows)] = own[...] + twin[...].astype(jnp.float32)

    @pl.when((z == 0) | (z == n_z - 1))
    def _():
        a_copies = [
            pltpu.make_async_copy(a_own[j], a_buf.at[j], a_sems.at[j]) for j in range(n_v)
        ]
        copies = [
            pltpu.make_async_copy(
                arrays[i], units.at[pl.ds(i * len(partners), len(partners))], sems.at[i]
            )
            for i in range(CORES)
        ]
        for copy in copies + a_copies:
            copy.start()
        total[rows] = jnp.zeros_like(total[rows])
        for copy in copies:
            copy.wait()
        n_units = CORES * len(partners)
        read_notes(units, n_units, cap, rows, notes_wide, notes, note_sem)
        for copy in a_copies:
            copy.wait()

        def one(i, carry):
            j = lax.rem(i, len(partners)) + partners[0]
            add_unit(i, j, cap, rows, a_buf, units, notes, total)
            return carry

        lax.fori_loop(0, n_units, one, 0)

    for o in range(live.shape[0]):
        for c in range(live.shape[1]):
            here = pl.ds(o * tile, tile)
            at = (here, pl.ds(c * tile, tile))
            kept = live[o, c].astype(jnp.float32)
            amps = amplitudes[at].astype(jnp.float32)
            masked = (amps * kept).astype(jnp.bfloat16).astype(jnp.float32)
            denominator = occupied[here, :] - virtual[:, pl.ds(c * tile, tile)]
            rest = (
                driver[at].astype(jnp.float32) + total[c, here] + denominator * amps
            ) * kept
            residual[at] = rest
            new[at] = (masked - rest / denominator).astype(new.dtype)


def on_device(
    amplitudes,
    tile_live,
    integrals,
    integral_columns,
    driver_terms,
    occupied_energy,
    virtual_energy,
):
    n_rows, width = amplitudes.shape
    rows, slots, tile, _ = integrals.shape
    n_v, n_o = lax.axis_size("vpair"), lax.axis_size("opair")
    n_z = n_o // CORES
    cap = -(-(rows * slots) // n_v)
    height = cap * tile + NOTE_ROWS
    dtype = integrals.dtype
    in_smem = pl.BlockSpec(memory_space=pltpu.SMEM)
    in_vmem = pl.BlockSpec(memory_space=pltpu.VMEM)
    anywhere = pl.BlockSpec(memory_space=pl.ANY)
    params = pltpu.CompilerParams(vmem_limit_bytes=VMEM_BYTES)

    *parcels, masked = pl.pallas_call(
        functools.partial(pack_kernel, n_v, cap),
        out_shape=[jax.ShapeDtypeStruct((1, height, tile), dtype)] * n_v
        + [jax.ShapeDtypeStruct(amplitudes.shape, amplitudes.dtype)],
        in_specs=[in_smem, in_smem, in_vmem, in_vmem],
        out_specs=[in_vmem] * (n_v + 1),
        scratch_shapes=[pltpu.SMEM((n_v * cap,), jnp.int32)] * 2,
        compiler_params=params,
        name="pack",
    )(integral_columns.T, tile_live, integrals, amplitudes)

    def across_v(value, j):
        return lax.ppermute(value, "vpair", [(i, i ^ j) for i in range(n_v)]) if j else value

    def across_core(value):
        return lax.ppermute(value, "opair", [(i, i ^ 1) for i in range(n_o)])

    def swap_z(value, odd):
        pairs = []
        for z in range(n_z):
            partner = ((z + odd) ^ 1) - odd
            for core in range(CORES):
                target = (partner, core) if 0 <= partner < n_z else (z, core ^ 1)
                pairs.append((z * CORES + core, target[0] * CORES + target[1]))
        return lax.ppermute(value, "opair", pairs)

    def next_hop(hops, hop):
        even = swap_z(hops["odd"][-1], 0)
        odd = swap_z(hops["even"][-1], 1) if hop < n_z - 2 else None
        return even, odd

    def add_hop(hops, even, odd):
        hops["even"].append(even)
        if odd is not None:
            hops["odd"].append(odd)

    others = list(range(1, n_v))
    near = {"even": [parcels[0]], "odd": [parcels[0]]}
    arrived = [across_v(parcels[j], j) for j in others]
    even, odd = next_hop(near, 0)
    start, even, odd, masked = lax.optimization_barrier(
        (jnp.concatenate(arrived), even, odd, masked)
    )
    add_hop(near, even, odd)
    far = {"even": [start], "odd": [start]}
    own_a = [masked]
    share = -(-len(others) // (n_z - 2))
    for hop in range(n_z - 2):
        far_even, far_odd = next_hop(far, hop)
        near_even, near_odd = next_hop(near, hop + 1)
        near_even, near_odd, masked = lax.optimization_barrier((near_even, near_odd, masked))
        some_a = [across_v(masked, j) for j in others[hop * share : (hop + 1) * share]]
        far_even, far_odd, near_even, near_odd, some_a = lax.optimization_barrier(
            (far_even, far_odd, near_even, near_odd, some_a)
        )
        add_hop(far, far_even, far_odd)
        add_hop(near, near_even, near_odd)
        own_a += some_a
    last, _ = next_hop(far, n_z - 2)
    arrays, layout = [], []
    for hops, partners in ((near, [0]), (far, others)):
        arrays += [hops["even"][0], *hops["even"][1:], *hops["odd"][1:]]
        layout += [("own", 0, partners)]
        layout += [("even", hop, partners) for hop in range(len(hops["even"]) - 1)]
        layout += [("odd", hop, partners) for hop in range(len(hops["odd"]) - 1)]
    twin_a = [across_core(value) for value in own_a]
    n_units = sum(len(partners) for _, _, partners in layout)

    own, twin, occupied = pl.pallas_call(
        functools.partial(ladder_kernel, n_v, n_z, cap, rows, layout),
        out_shape=[
            jax.ShapeDtypeStruct((rows, n_rows, tile), jnp.float32),
            jax.ShapeDtypeStruct((rows, n_rows, tile), jnp.bfloat16),
            jax.ShapeDtypeStruct((n_rows, tile), jnp.float32),
        ],
        in_specs=[in_vmem] + [anywhere] * (2 * n_v + len(arrays)),
        out_specs=[in_vmem] * 3,
        scratch_shapes=[
            pltpu.VMEM((n_v, CORES * n_rows, width), amplitudes.dtype),
            pltpu.VMEM((n_units, height, tile), dtype),
            pltpu.VMEM((n_units, tile), jnp.int32),
            pltpu.SMEM((n_units, tile), jnp.int32),
            pltpu.SMEM((2, n_units + 1), jnp.int32),
            pltpu.VMEM((rows + 1, CORES * n_rows, tile), jnp.float32),
            pltpu.SemaphoreType.DMA((2 * n_v,)),
            pltpu.SemaphoreType.DMA((len(arrays),)),
            pltpu.SemaphoreType.DMA,
        ],
        compiler_params=params,
        cost_estimate=pl.CostEstimate(
            flops=8 * n_units * cap * n_rows * tile * tile * CORES,
            bytes_accessed=16 * 1024 * 1024,
            transcendentals=0,
        ),
        name="ladder",
    )(occupied_energy.reshape(-1, tile), *own_a, *twin_a, *arrays)
    twin, last = lax.optimization_barrier((across_core(twin), last))
    n_last = CORES * len(others)

    return pl.pallas_call(
        functools.partial(update_kernel, n_v, n_z, cap, others),
        out_shape=[
            jax.ShapeDtypeStruct((n_rows, width), jnp.bfloat16),
            jax.ShapeDtypeStruct((n_rows, width), jnp.float32),
        ],
        in_specs=[in_smem] + [in_vmem] * 6 + [anywhere] * (n_v + CORES),
        out_specs=[in_vmem] * 2,
        scratch_shapes=[
            pltpu.VMEM((n_v, n_rows, width), amplitudes.dtype),
            pltpu.VMEM((n_last, height, tile), dtype),
            pltpu.VMEM((n_last, tile), jnp.int32),
            pltpu.SMEM((n_last, tile), jnp.int32),
            pltpu.VMEM((rows + 1, n_rows, tile), jnp.float32),
            pltpu.SemaphoreType.DMA((n_v,)),
            pltpu.SemaphoreType.DMA((CORES,)),
            pltpu.SemaphoreType.DMA,
        ],
        compiler_params=params,
        name="update",
    )(
        tile_live,
        amplitudes,
        driver_terms,
        own,
        twin,
        occupied,
        virtual_energy.reshape(1, width),
        *own_a,
        last,
        across_core(last),
    )


def solution(mesh):
    in_specs = (
        P("opair", "vpair"),
        P("opair", "vpair"),
        P("vpair", "opair", None, None),
        P("vpair", "opair"),
        P("opair", "vpair"),
        P("opair"),
        P("vpair"),
    )
    out_specs = (P("opair", "vpair"), P("opair", "vpair"))
    return jax.shard_map(
        on_device, mesh=mesh, in_specs=in_specs, out_specs=out_specs, check_vma=False
    )
```

```python
import functools
import math

import jax
import jax.numpy as jnp
from jax import lax
from jax.experimental import pallas as pl
from jax.experimental.pallas import tpu as pltpu
from jax.sharding import PartitionSpec as P

SPARE_VMEM = 4 * 1024 * 1024
CORES = 2
NOTE_ROWS = 16
FIRST_FLOPS = 10**8
SECOND_FLOPS = 10**9


def pack_kernel(n_v, cap, columns, live, integrals, amplitudes, *refs):
    parcels, (masked, origin, codes, tiles, amps, sems) = refs[:n_v], refs[n_v:]
    rows, slots, tile, _ = integrals.shape
    me = lax.axis_index("vpair")
    copies = [
        pltpu.make_async_copy(integrals, tiles, sems.at[0]),
        pltpu.make_async_copy(amplitudes, amps, sems.at[1]),
    ]
    for copy in copies:
        copy.start()
    counts = [jnp.int32(0)] * n_v
    for i in range(n_v * cap):
        origin[i] = 0
        codes[i] = -1
    for row in range(rows):
        for slot in range(slots):
            column = columns[slot, row]
            partner = lax.div(column, rows) ^ me
            place = counts[0]
            for j in range(1, n_v):
                place = jnp.where(partner == j, counts[j], place)
            counts = [counts[j] + (partner == j).astype(jnp.int32) for j in range(n_v)]
            at = partner * cap + place
            origin[at] = row * slots + slot
            codes[at] = row * rows + lax.rem(column, rows)
    copies[0].wait()
    lane = lax.broadcasted_iota(jnp.int32, (NOTE_ROWS, tile), 1)
    for j in range(n_v):
        note = jnp.full((NOTE_ROWS, tile), -1, jnp.int32)
        for k in range(cap):
            entry = origin[j * cap + k]
            parcels[j][0, pl.ds(k * tile, tile)] = tiles[
                lax.div(entry, slots), lax.rem(entry, slots)
            ]
            note = jnp.where(lane == k, codes[j * cap + k], note)
        parcels[j][0, pl.ds(cap * tile, NOTE_ROWS)] = note.astype(jnp.float32).astype(
            integrals.dtype
        )
    copies[1].wait()
    for o in range(live.shape[0]):
        for c in range(live.shape[1]):
            at = (pl.ds(o * tile, tile), pl.ds(c * tile, tile))
            kept = live[o, c].astype(jnp.float32)
            masked[at] = (amps[at].astype(jnp.float32) * kept).astype(masked.dtype)


def fetch(arrays, units, note_buf, unit_sems, note_sems):
    tile = units.shape[-1]
    bounds, first = [], 0
    for array in arrays:
        bounds.append(pl.ds(first, array.shape[0]))
        first += array.shape[0]
    note_rows = pl.ds(units.shape[1] - NOTE_ROWS, NOTE_ROWS)
    note_copies = [
        pltpu.make_async_copy(array.at[:, note_rows], note_buf.at[part], note_sems.at[i])
        for i, (array, part) in enumerate(zip(arrays, bounds))
    ]
    unit_copies = [
        pltpu.make_async_copy(array, units.at[part], unit_sems.at[i])
        for i, (array, part) in enumerate(zip(arrays, bounds))
    ]
    for copy in note_copies + unit_copies:
        copy.start()
    return note_copies, unit_copies


def read_notes(note_copies, note_buf, notes_wide, notes, sem):
    for copy in note_copies:
        copy.wait()
    for u in range(note_buf.shape[0]):
        notes_wide[pl.ds(u, 1)] = note_buf[u].astype(jnp.float32).astype(jnp.int32)[:1]
    copy = pltpu.make_async_copy(notes_wide, notes, sem)
    copy.start()
    copy.wait()


def clear_pairs(pairs):
    pairs[...] = jnp.zeros_like(pairs)


def add_unit(unit, j, cap, rows, amps, units, notes, pairs, total):
    tile = units.shape[-1]

    def place(k):
        code = notes[unit, k]
        used = code >= 0
        row = jnp.where(used, lax.div(code, rows), 0)
        column = jnp.where(used, lax.rem(code, rows), rows)
        return amps[j, :, pl.ds(pl.multiple_of(row * tile, tile), tile)], column

    for k in range(0, cap - 1, 2):
        pair = pairs.at[k // 2]
        pair[pl.ds(0, tile), pl.ds(0, tile)] = units[unit, pl.ds(k * tile, tile)]
        pair[pl.ds(tile, tile), pl.ds(tile, tile)] = units[unit, pl.ds((k + 1) * tile, tile)]
        (left, first), (right, second) = place(k), place(k + 1)
        both = jnp.dot(
            jnp.concatenate([left, right], axis=1),
            pair[...],
            preferred_element_type=jnp.float32,
        )
        total[first] += both[:, :tile]
        total[second] += both[:, tile:]
    if cap % 2:
        left, column = place(cap - 1)
        total[column] += jnp.dot(
            left,
            units[unit, pl.ds((cap - 1) * tile, tile)],
            preferred_element_type=jnp.float32,
        )


def ladder_kernel(cap, layout, amps, *refs):
    arrays, (total, units, note_buf, notes_wide, notes, pairs, *sems) = (
        refs[: len(layout)],
        refs[len(layout) :],
    )
    rows = total.shape[0] - 1
    note_copies, unit_copies = fetch(arrays, units, note_buf, sems[0], sems[1])
    clear_pairs(pairs)
    total[...] = jnp.zeros_like(total)
    read_notes(note_copies, note_buf, notes_wide, notes, sems[2])
    first = 0
    for copy, partners in zip(unit_copies, layout):
        copy.wait()

        def one(i, carry, first=first, partners=partners):
            add_unit(first + i, partners[0] + i, cap, rows, amps, units, notes, pairs, total)
            return carry

        lax.fori_loop(0, len(partners), one, 0)
        first += len(partners)


def first_ladder_kernel(cap, layout, occupied, *refs):
    n_in = 1 + len(layout)
    occupied_out = refs[n_in + 1]
    tile = occupied_out.shape[-1]
    for o in range(occupied.shape[0]):
        wide = jnp.broadcast_to(occupied[pl.ds(o, 1)], (tile, tile))
        occupied_out[pl.ds(o * tile, tile)] = wide.T
    ladder_kernel(cap, layout, *refs[: n_in + 1], *refs[n_in + 2 :])


def second_ladder_kernel(cap, layout, before, *refs):
    n_in = 1 + len(layout)
    own, twin, total = refs[n_in : n_in + 3]
    ladder_kernel(cap, layout, *refs[:n_in], total, *refs[n_in + 3 :])
    rows, n_rows, _ = own.shape
    own[...] = before[:rows, :n_rows] + total[:rows, :n_rows]
    twin[...] = (before[:rows, n_rows:] + total[:rows, n_rows:]).astype(twin.dtype)


def update_kernel(
    cap, live, amplitudes, driver, own, twin, occupied, virtual, *refs
):
    amps_all, *arrays = refs[: 1 + CORES]
    new, residual, a_buf, units, note_buf, notes_wide, notes, pairs, total = refs[1 + CORES : -4]
    a_sem, *sems = refs[-4:]
    group, n_rows, tile = own.shape
    rows = live.shape[1]
    step = pl.program_id(0)
    n_a = a_buf.shape[0]

    @pl.when(step == 0)
    def _():
        total[...] = jnp.zeros_like(total)
        note_copies, unit_copies = fetch(arrays, units, note_buf, sems[0], sems[1])
        a_copy = pltpu.make_async_copy(
            amps_all.at[pl.ds(amps_all.shape[0] - n_a, n_a), pl.ds(0, n_rows)], a_buf, a_sem
        )
        a_copy.start()
        clear_pairs(pairs)
        read_notes(note_copies, note_buf, notes_wide, notes, sems[2])
        a_copy.wait()
        for copy in unit_copies:
            copy.wait()

        def one(i, carry):
            add_unit(i, lax.rem(i, n_a), cap, rows, a_buf, units, notes, pairs, total)
            return carry

        lax.fori_loop(0, CORES * n_a, one, 0)

    for o in range(live.shape[0]):
        for c in range(group):
            here = pl.ds(o * tile, tile)
            at = (here, pl.ds(c * tile, tile))
            kept = live[o, step * group + c].astype(jnp.float32)
            amps = amplitudes[at].astype(jnp.float32)
            masked = (amps * kept).astype(jnp.bfloat16).astype(jnp.float32)
            denominator = occupied[here, :] - virtual[:, pl.ds(c * tile, tile)]
            ladder = (
                own[c, here] + twin[c, here].astype(jnp.float32) + total[step * group + c, here]
            )
            rest = (driver[at].astype(jnp.float32) + ladder + denominator * amps) * kept
            residual[at] = rest
            new[at] = (masked - rest / denominator).astype(new.dtype)


def on_device(
    amplitudes,
    tile_live,
    integrals,
    integral_columns,
    driver_terms,
    occupied_energy,
    virtual_energy,
):
    n_rows, width = amplitudes.shape
    rows, slots, tile, _ = integrals.shape
    n_v, n_o = lax.axis_size("vpair"), lax.axis_size("opair")
    n_z = n_o // CORES
    cap = -(-(rows * slots) // n_v)
    height = cap * tile + NOTE_ROWS
    dtype = integrals.dtype
    in_smem = pl.BlockSpec(memory_space=pltpu.SMEM)
    in_vmem = pl.BlockSpec(memory_space=pltpu.VMEM)
    anywhere = pl.BlockSpec(memory_space=pl.ANY)
    in_hbm = pl.BlockSpec(memory_space=pltpu.HBM)

    def params(*buffers):
        size = sum(math.prod(shape) * jnp.dtype(kind).itemsize for shape, kind in buffers)
        return pltpu.CompilerParams(vmem_limit_bytes=size + SPARE_VMEM)

    parcel = (1, height, tile)
    *parcels, masked = pl.pallas_call(
        functools.partial(pack_kernel, n_v, cap),
        out_shape=[jax.ShapeDtypeStruct(parcel, dtype)] * n_v
        + [jax.ShapeDtypeStruct(amplitudes.shape, amplitudes.dtype)],
        in_specs=[in_smem, in_smem, in_hbm, in_hbm],
        out_specs=[in_vmem] * (n_v + 1),
        scratch_shapes=[pltpu.SMEM((n_v * cap,), jnp.int32)] * 2
        + [
            pltpu.VMEM(integrals.shape, dtype),
            pltpu.VMEM(amplitudes.shape, dtype),
            pltpu.SemaphoreType.DMA((2,)),
        ],
        compiler_params=params(
            (integrals.shape, dtype), ((n_v, *parcel), dtype), ((2, n_rows, width), dtype)
        ),
        name="pack",
    )(integral_columns.T, tile_live, integrals, amplitudes)

    def across_v(value, j):
        name = "amplitudes" if value.ndim == 2 else "parcels"
        with jax.named_scope(f"{name}_from_partner_{j}"):
            return lax.ppermute(value, "vpair", [(i, i ^ j) for i in range(n_v)])

    def across_core(value):
        return lax.ppermute(value, "opair", [(i, i ^ 1) for i in range(n_o)])

    def next_on_ring(value, name):
        ring = [*range(0, n_z, 2), *range(n_z - 1 - n_z % 2, 0, -2)]
        pairs = [
            (source * CORES + core, target * CORES + core)
            for source, target in zip(ring, ring[1:] + ring[:1])
            for core in range(CORES)
        ]
        with jax.named_scope(name):
            return lax.ppermute(value, "opair", pairs)

    def join(values):
        return jnp.concatenate(values) if len(values) > 1 else values[0]

    def after(values, others):
        return lax.optimization_barrier((values, others))[0]

    others = list(range(1, n_v))
    groups = {"near": [0], "early": others[: n_v // 2 - 1], "late": others[n_v // 2 - 1 :]}
    arrived = {0: parcels[0]} | {j: across_v(parcels[j], j) for j in others}
    hops = {name: [join([arrived[j] for j in groups[name]])] for name in groups}
    for hop in range(1, n_z):
        for name in groups:
            hops[name].append(next_on_ring(hops[name][-1], f"{name}_hop_{hop}"))

    a_parts = {0: masked}
    ready = after(masked, hops["late"][0])
    for j in others:
        a_parts[j] = across_v(ready, j)
    with jax.named_scope("twin_amplitudes"):
        a_twins = {j: across_core(a_parts[j]) for j in range(n_v)}
    amps = jnp.stack([jnp.concatenate([a_parts[j], a_twins[j]]) for j in range(n_v)])

    sums = (rows + 1, CORES * n_rows, tile)
    pairs = (max(cap // 2, 1), 2 * tile, 2 * tile)

    def ladder_call(kernel, found, before, out_shape, extra_scratch, flops, name):
        arrays, layout = [hops[name][hop] for name, hop in found], [groups[name] for name, _ in found]
        n_units = sum(len(partners) for partners in layout)
        units = (n_units, height, tile)
        return pl.pallas_call(
            functools.partial(kernel, cap, layout),
            out_shape=out_shape,
            in_specs=[in_vmem, in_vmem] + [anywhere] * len(arrays),
            out_specs=[in_vmem] * len(out_shape),
            scratch_shapes=extra_scratch
            + [
                pltpu.VMEM(units, dtype),
                pltpu.VMEM((n_units, NOTE_ROWS, tile), dtype),
                pltpu.VMEM((n_units, tile), jnp.int32),
                pltpu.SMEM((n_units, tile), jnp.int32),
                pltpu.VMEM(pairs, dtype),
                pltpu.SemaphoreType.DMA((len(arrays),)),
                pltpu.SemaphoreType.DMA((len(arrays),)),
                pltpu.SemaphoreType.DMA,
            ],
            compiler_params=params(
                (units, dtype), (sums, jnp.float32), (sums, jnp.float32), (amps.shape, dtype)
            ),
            cost_estimate=pl.CostEstimate(
                flops=flops,
                bytes_accessed=1024 * 1024,
                transcendentals=0,
            ),
            name=name,
        )(before, amps, *arrays)

    tail = [("late", n_z - 2), ("near", n_z - 1), ("early", n_z - 1)]
    head = [(name, hop) for hop in range(n_z - 1) for name in groups if (name, hop) not in tail]
    total, occupied = ladder_call(
        first_ladder_kernel,
        head,
        occupied_energy.reshape(-1, tile),
        [
            jax.ShapeDtypeStruct(sums, jnp.float32),
            jax.ShapeDtypeStruct((n_rows, tile), jnp.float32),
        ],
        [],
        FIRST_FLOPS,
        "ladder_first",
    )
    own, twin = ladder_call(
        second_ladder_kernel,
        tail,
        total,
        [
            jax.ShapeDtypeStruct((rows, n_rows, tile), jnp.float32),
            jax.ShapeDtypeStruct((rows, n_rows, tile), jnp.bfloat16),
        ],
        [pltpu.VMEM(sums, jnp.float32)],
        SECOND_FLOPS,
        "ladder_second",
    )
    last, behind = after(hops["late"][-1], twin), groups["late"]
    twin = across_core(twin)

    group = 2 if rows % 2 == 0 else 1
    a_buf = (len(behind), n_rows, width)
    units = (CORES * len(behind), height, tile)
    sums = (rows + 1, n_rows, tile)
    block = pl.BlockSpec((n_rows, group * tile), lambda c: (0, c))
    tiles = pl.BlockSpec((group, n_rows, tile), lambda c: (c, 0, 0))
    return pl.pallas_call(
        functools.partial(update_kernel, cap),
        grid=(rows // group,),
        out_shape=[
            jax.ShapeDtypeStruct((n_rows, width), jnp.bfloat16),
            jax.ShapeDtypeStruct((n_rows, width), jnp.float32),
        ],
        in_specs=[
            in_smem,
            block,
            block,
            tiles,
            tiles,
            pl.BlockSpec((n_rows, tile), lambda c: (0, 0)),
            pl.BlockSpec((1, group * tile), lambda c: (0, c)),
        ]
        + [anywhere] * (1 + CORES),
        out_specs=[block, block],
        scratch_shapes=[
            pltpu.VMEM(a_buf, amplitudes.dtype),
            pltpu.VMEM(units, dtype),
            pltpu.VMEM((units[0], NOTE_ROWS, tile), dtype),
            pltpu.VMEM((units[0], tile), jnp.int32),
            pltpu.SMEM((units[0], tile), jnp.int32),
            pltpu.VMEM(pairs, dtype),
            pltpu.VMEM(sums, jnp.float32),
            pltpu.SemaphoreType.DMA,
            pltpu.SemaphoreType.DMA((CORES,)),
            pltpu.SemaphoreType.DMA((CORES,)),
            pltpu.SemaphoreType.DMA,
        ],
        compiler_params=params(
            (a_buf, dtype), (units, dtype), (sums, jnp.float32), (sums, jnp.float32)
        ),
        name="update",
    )(
        tile_live,
        amplitudes,
        driver_terms,
        own,
        twin,
        occupied,
        virtual_energy.reshape(1, width),
        amps,
        last,
        across_core(last),
    )


def solution(mesh):
    in_specs = (
        P("opair", "vpair"),
        P("opair", "vpair"),
        P("vpair", "opair", None, None),
        P("vpair", "opair"),
        P("opair", "vpair"),
        P("opair"),
        P("vpair"),
    )
    out_specs = (P("opair", "vpair"), P("opair", "vpair"))
    return jax.shard_map(
        on_device, mesh=mesh, in_specs=in_specs, out_specs=out_specs, check_vma=False
    )
```

```python
import functools
import math

import jax
import jax.numpy as jnp
from jax import lax
from jax.experimental import pallas as pl
from jax.experimental.pallas import tpu as pltpu
from jax.sharding import PartitionSpec as P

SPARE_VMEM = 4 * 1024 * 1024
ALL_VMEM = 60 * 1024 * 1024
CORES = 2
NOTE_ROWS = 16
FIRST_FLOPS = 10**8
SECOND_FLOPS = 10**9


def pack_kernel(n_v, cap, columns, integrals, *refs):
    parcels, (origin, codes, tiles, sem) = refs[:n_v], refs[n_v:]
    rows, slots, tile, _ = integrals.shape
    me = lax.axis_index("vpair")
    copy = pltpu.make_async_copy(integrals, tiles, sem)
    copy.start()
    counts = [jnp.int32(0)] * n_v
    for i in range(n_v * cap):
        origin[i] = 0
        codes[i] = -1
    for row in range(rows):
        for slot in range(slots):
            column = columns[slot, row]
            partner = lax.div(column, rows) ^ me
            place = counts[0]
            for j in range(1, n_v):
                place = jnp.where(partner == j, counts[j], place)
            counts = [counts[j] + (partner == j).astype(jnp.int32) for j in range(n_v)]
            at = partner * cap + place
            origin[at] = row * slots + slot
            codes[at] = row * rows + lax.rem(column, rows)
    copy.wait()
    lane = lax.broadcasted_iota(jnp.int32, (NOTE_ROWS, tile), 1)
    for j in range(n_v):
        note = jnp.full((NOTE_ROWS, tile), -1, jnp.int32)
        for k in range(cap):
            entry = origin[j * cap + k]
            parcels[j][0, pl.ds(k * tile, tile)] = tiles[
                lax.div(entry, slots), lax.rem(entry, slots)
            ]
            note = jnp.where(lane == k, codes[j * cap + k], note)
        parcels[j][0, pl.ds(cap * tile, NOTE_ROWS)] = note.astype(jnp.float32).astype(
            integrals.dtype
        )


def mask_kernel(live, amplitudes, masked):
    tile = amplitudes.shape[1] // live.shape[1]
    for o in range(live.shape[0]):
        for c in range(live.shape[1]):
            at = (pl.ds(o * tile, tile), pl.ds(c * tile, tile))
            kept = live[o, c].astype(jnp.float32)
            masked[at] = (amplitudes[at].astype(jnp.float32) * kept).astype(masked.dtype)


def read_notes(arrays, notes_wide, notes, sem):
    unit = 0
    for array in arrays:
        _, height, _ = array.shape
        for member in range(array.shape[0]):
            note = array[member, pl.ds(height - NOTE_ROWS, NOTE_ROWS)]
            notes_wide[pl.ds(unit, 1)] = note.astype(jnp.float32).astype(jnp.int32)[:1]
            unit += 1
    copy = pltpu.make_async_copy(notes_wide, notes, sem)
    copy.start()
    return copy


def clear_pairs(pairs):
    pairs[...] = jnp.zeros_like(pairs)


def add_unit(array, member, unit, j, n_rows, cap, rows, amps, notes, pairs, total):
    tile = array.shape[-1]

    def place(k):
        code = notes[unit, k]
        used = code >= 0
        row = jnp.where(used, lax.div(code, rows), 0)
        column = jnp.where(used, lax.rem(code, rows), rows)
        lanes = pl.ds(pl.multiple_of(row * tile, tile), tile)
        return amps[j, pl.ds(0, n_rows), lanes], column

    for k in range(0, cap - 1, 2):
        pair = pairs.at[k // 2]
        pair[pl.ds(0, tile), pl.ds(0, tile)] = array[member, pl.ds(k * tile, tile)]
        pair[pl.ds(tile, tile), pl.ds(tile, tile)] = array[member, pl.ds((k + 1) * tile, tile)]
        (left, first), (right, second) = place(k), place(k + 1)
        both = jnp.dot(
            jnp.concatenate([left, right], axis=1),
            pair[...],
            preferred_element_type=jnp.float32,
        )
        total[first] += both[:, :tile]
        total[second] += both[:, tile:]
    if cap % 2:
        left, column = place(cap - 1)
        total[column] += jnp.dot(
            left,
            array[member, pl.ds((cap - 1) * tile, tile)],
            preferred_element_type=jnp.float32,
        )


def add_arrays(arrays, layout, cap, rows, amps, notes_wide, notes, pairs, total, sem):
    copy = read_notes(arrays, notes_wide, notes, sem)
    pairs[...] = jnp.zeros_like(pairs)
    total[...] = jnp.zeros_like(total)
    copy.wait()
    unit = 0
    for array, partners in zip(arrays, layout):

        def one(i, carry, unit=unit, array=array, partners=partners):
            add_unit(
                array, i, unit + i, partners[0] + i, total.shape[1], cap, rows, amps, notes, pairs, total
            )
            return carry

        lax.fori_loop(0, len(partners), one, 0)
        unit += len(partners)


def first_ladder_kernel(cap, layout, occupied, amps, *refs):
    arrays, (total, occupied_out, notes_wide, notes, pairs, sem) = (
        refs[: len(layout)],
        refs[len(layout) :],
    )
    rows = total.shape[0] - 1
    add_arrays(arrays, layout, cap, rows, amps, notes_wide, notes, pairs, total, sem)
    tile = occupied_out.shape[-1]
    for o in range(occupied.shape[0]):
        wide = jnp.broadcast_to(occupied[pl.ds(o, 1)], (tile, tile))
        occupied_out[pl.ds(o * tile, tile)] = wide.T


def second_ladder_kernel(cap, layout, before, amps, *refs):
    arrays, (own, twin, total, notes_wide, notes, pairs, sem) = (
        refs[: len(layout)],
        refs[len(layout) :],
    )
    rows, n_rows, _ = own.shape
    add_arrays(arrays, layout, cap, rows, amps, notes_wide, notes, pairs, total, sem)
    own[...] = before[:rows, :n_rows] + total[:rows, :n_rows]
    twin[...] = (before[:rows, n_rows:] + total[:rows, n_rows:]).astype(twin.dtype)


def update_kernel(cap, partners, live, amplitudes, driver, own, twin, occupied, virtual, *refs):
    amps, *arrays = refs[: 1 + CORES]
    new, residual, new_buf, residual_buf, notes_wide, notes, pairs, total, sem, sems = refs[
        1 + CORES :
    ]
    rows, _, tile = own.shape
    layout = [partners] * CORES
    add_arrays(arrays, layout, cap, rows, amps, notes_wide, notes, pairs, total, sem)
    copies = []
    for c in range(rows):
        lanes = pl.ds(c * tile, tile)
        for o in range(live.shape[0]):
            here = pl.ds(o * tile, tile)
            at = (here, lanes)
            kept = live[o, c].astype(jnp.float32)
            plain = amplitudes[at].astype(jnp.float32)
            masked = (plain * kept).astype(jnp.bfloat16).astype(jnp.float32)
            denominator = occupied[here, :] - virtual[:, lanes]
            ladder = own[c, here] + twin[c, here].astype(jnp.float32) + total[c, here]
            rest = (driver[at].astype(jnp.float32) + ladder + denominator * plain) * kept
            residual_buf[at] = rest
            new_buf[at] = (masked - rest / denominator).astype(new.dtype)
        for i, (source, target) in enumerate(((new_buf, new), (residual_buf, residual))):
            copies.append(
                pltpu.make_async_copy(source.at[:, lanes], target.at[:, lanes], sems.at[i, c])
            )
            copies[-1].start()
    for copy in copies:
        copy.wait()


def on_device(
    amplitudes,
    tile_live,
    integrals,
    integral_columns,
    driver_terms,
    occupied_energy,
    virtual_energy,
):
    n_rows, width = amplitudes.shape
    rows, slots, tile, _ = integrals.shape
    n_v, n_o = lax.axis_size("vpair"), lax.axis_size("opair")
    n_z = n_o // CORES
    cap = -(-(rows * slots) // n_v)
    height = cap * tile + NOTE_ROWS
    dtype = integrals.dtype
    in_smem = pl.BlockSpec(memory_space=pltpu.SMEM)
    in_vmem = pl.BlockSpec(memory_space=pltpu.VMEM)
    anywhere = pl.BlockSpec(memory_space=pl.ANY)
    in_hbm = pl.BlockSpec(memory_space=pltpu.HBM)

    def params(*buffers):
        size = sum(math.prod(shape) * jnp.dtype(kind).itemsize for shape, kind in buffers)
        return pltpu.CompilerParams(vmem_limit_bytes=size + SPARE_VMEM)

    parcel = (1, height, tile)
    parcels = pl.pallas_call(
        functools.partial(pack_kernel, n_v, cap),
        out_shape=[jax.ShapeDtypeStruct(parcel, dtype)] * n_v,
        in_specs=[in_smem, in_hbm],
        out_specs=[in_vmem] * n_v,
        scratch_shapes=[pltpu.SMEM((n_v * cap,), jnp.int32)] * 2
        + [pltpu.VMEM(integrals.shape, dtype), pltpu.SemaphoreType.DMA],
        compiler_params=pltpu.CompilerParams(vmem_limit_bytes=ALL_VMEM),
        name="pack",
    )(integral_columns.T, integrals)
    masked = pl.pallas_call(
        mask_kernel,
        out_shape=jax.ShapeDtypeStruct(amplitudes.shape, amplitudes.dtype),
        in_specs=[in_smem, in_vmem],
        out_specs=in_vmem,
        compiler_params=params(((4, n_rows, width), dtype)),
        name="mask",
    )(tile_live, amplitudes)

    def across_v(value, j):
        name = "amplitudes" if value.ndim == 2 else "parcels"
        with jax.named_scope(f"{name}_from_partner_{j}"):
            return lax.ppermute(value, "vpair", [(i, i ^ j) for i in range(n_v)])

    def across_core(value):
        return lax.ppermute(value, "opair", [(i, i ^ 1) for i in range(n_o)])

    def next_on_ring(value, name):
        ring = [*range(0, n_z, 2), *range(n_z - 1 - n_z % 2, 0, -2)]
        pairs = [
            (source * CORES + core, target * CORES + core)
            for source, target in zip(ring, ring[1:] + ring[:1])
            for core in range(CORES)
        ]
        with jax.named_scope(name):
            return lax.ppermute(value, "opair", pairs)

    def join(values):
        return jnp.concatenate(values) if len(values) > 1 else values[0]

    def after(values, others):
        return lax.optimization_barrier((values, others))[0]

    others = list(range(1, n_v))
    groups = {"near": [0], "early": others[: n_v // 2 - 1], "late": others[n_v // 2 - 1 :]}
    arrived = {0: parcels[0]} | {j: across_v(parcels[j], j) for j in others}
    hops = {name: [join([arrived[j] for j in groups[name]])] for name in groups}
    groups["first"] = groups["near"] + groups["early"]
    for name in ("near", "early", "late"):
        hops[name].append(next_on_ring(hops[name][0], f"{name}_hop_1"))
    hops["first"] = [None, join([hops["near"][1], hops["early"][1]])]
    for hop in range(2, n_z):
        for name in ("first", "late"):
            hops[name].append(next_on_ring(hops[name][-1], f"{name}_hop_{hop}"))

    a_parts = {0: masked}
    ready = after(masked, hops["late"][0])
    for j in others:
        a_parts[j] = across_v(ready, j)
    a_parts = after(a_parts, (hops["first"][2], hops["late"][2]))
    own_a = jnp.stack([a_parts[j] for j in range(n_v)])
    with jax.named_scope("twin_amplitudes"):
        amps = jnp.concatenate([own_a, across_core(own_a)], axis=1)

    sums = (rows + 1, CORES * n_rows, tile)
    pairs = (max(cap // 2, 1), 2 * tile, 2 * tile)

    def ladder_call(kernel, found, before, out_shape, extra_scratch, flops, name):
        arrays, layout = [hops[name][hop] for name, hop in found], [groups[name] for name, _ in found]
        n_units = sum(len(partners) for partners in layout)
        return pl.pallas_call(
            functools.partial(kernel, cap, layout),
            out_shape=out_shape,
            in_specs=[in_vmem] * (2 + len(arrays)),
            out_specs=[in_vmem] * len(out_shape),
            scratch_shapes=extra_scratch
            + [
                pltpu.VMEM((n_units, tile), jnp.int32),
                pltpu.SMEM((n_units, tile), jnp.int32),
                pltpu.VMEM(pairs, dtype),
                pltpu.SemaphoreType.DMA,
            ],
            compiler_params=params(
                ((n_units, height, tile), dtype),
                (sums, jnp.float32),
                (sums, jnp.float32),
                (sums, jnp.float32),
                (amps.shape, dtype),
            ),
            cost_estimate=pl.CostEstimate(
                flops=flops,
                bytes_accessed=1024 * 1024,
                transcendentals=0,
            ),
            name=name,
        )(before, amps, *arrays)

    tail = [("late", n_z - 2), ("first", n_z - 1)]
    head = [("near", 0), ("early", 0), ("late", 0)]
    head += [("first", hop) for hop in range(1, n_z - 1)]
    head += [("late", hop) for hop in range(1, n_z - 2)]
    total, occupied = ladder_call(
        first_ladder_kernel,
        head,
        occupied_energy.reshape(-1, tile),
        [
            jax.ShapeDtypeStruct(sums, jnp.float32),
            jax.ShapeDtypeStruct((n_rows, tile), jnp.float32),
        ],
        [],
        FIRST_FLOPS,
        "ladder_first",
    )
    own, twin = ladder_call(
        second_ladder_kernel,
        tail,
        total,
        [
            jax.ShapeDtypeStruct((rows, n_rows, tile), jnp.float32),
            jax.ShapeDtypeStruct((rows, n_rows, tile), jnp.bfloat16),
        ],
        [pltpu.VMEM(sums, jnp.float32)],
        SECOND_FLOPS,
        "ladder_second",
    )
    last, behind = after(hops["late"][-1], twin), groups["late"]
    twin = across_core(twin)

    n_last = CORES * len(behind)
    sums = (rows + 1, n_rows, tile)
    return pl.pallas_call(
        functools.partial(update_kernel, cap, behind),
        out_shape=[
            jax.ShapeDtypeStruct((n_rows, width), jnp.bfloat16),
            jax.ShapeDtypeStruct((n_rows, width), jnp.float32),
        ],
        in_specs=[in_smem] + [in_vmem] * (7 + CORES),
        out_specs=[in_hbm] * 2,
        scratch_shapes=[
            pltpu.VMEM((n_rows, width), jnp.bfloat16),
            pltpu.VMEM((n_rows, width), jnp.float32),
            pltpu.VMEM((n_last, tile), jnp.int32),
            pltpu.SMEM((n_last, tile), jnp.int32),
            pltpu.VMEM(pairs, dtype),
            pltpu.VMEM(sums, jnp.float32),
            pltpu.SemaphoreType.DMA,
            pltpu.SemaphoreType.DMA((2, rows)),
        ],
        compiler_params=params(
            (amps.shape, dtype), ((n_last, height, tile), dtype), *[(sums, jnp.float32)] * 5
        ),
        name="update",
    )(
        tile_live,
        amplitudes,
        driver_terms,
        own,
        twin,
        occupied,
        virtual_energy.reshape(1, width),
        amps,
        last,
        across_core(last),
    )


def solution(mesh):
    in_specs = (
        P("opair", "vpair"),
        P("opair", "vpair"),
        P("vpair", "opair", None, None),
        P("vpair", "opair"),
        P("opair", "vpair"),
        P("opair"),
        P("vpair"),
    )
    out_specs = (P("opair", "vpair"), P("opair", "vpair"))
    return jax.shard_map(
        on_device, mesh=mesh, in_specs=in_specs, out_specs=out_specs, check_vma=False
    )
```

```python
import functools
import math

import jax
import jax.numpy as jnp
from jax import lax
from jax.experimental import pallas as pl
from jax.experimental.pallas import tpu as pltpu
from jax.sharding import PartitionSpec as P

SPARE_VMEM = 4 * 1024 * 1024
ALL_VMEM = 60 * 1024 * 1024
CORES = 2
NOTE_ROWS = 16
FIRST_FLOPS = 10**8
SECOND_FLOPS = 10**9


def pack_kernel(n_v, cap, columns, live, integrals, amplitudes, *refs):
    parcels, (masked, origin, codes) = refs[:n_v], refs[n_v:]
    rows, slots, tile, _ = integrals.shape
    me = lax.axis_index("vpair")
    counts = [jnp.int32(0)] * n_v
    for i in range(n_v * cap):
        origin[i] = 0
        codes[i] = -1
    for row in range(rows):
        for slot in range(slots):
            column = columns[slot, row]
            partner = lax.div(column, rows) ^ me
            place = counts[0]
            for j in range(1, n_v):
                place = jnp.where(partner == j, counts[j], place)
            counts = [counts[j] + (partner == j).astype(jnp.int32) for j in range(n_v)]
            at = partner * cap + place
            origin[at] = row * slots + slot
            codes[at] = row * rows + lax.rem(column, rows)
    lane = lax.broadcasted_iota(jnp.int32, (NOTE_ROWS, tile), 1)
    for j in range(n_v):
        note = jnp.full((NOTE_ROWS, tile), -1, jnp.int32)
        for k in range(cap):
            entry = origin[j * cap + k]
            parcels[j][0, pl.ds(k * tile, tile)] = integrals[
                lax.div(entry, slots), lax.rem(entry, slots)
            ]
            note = jnp.where(lane == k, codes[j * cap + k], note)
        parcels[j][0, pl.ds(cap * tile, NOTE_ROWS)] = note.astype(jnp.float32).astype(
            integrals.dtype
        )
    for o in range(live.shape[0]):
        for c in range(live.shape[1]):
            at = (pl.ds(o * tile, tile), pl.ds(c * tile, tile))
            kept = live[o, c].astype(jnp.float32)
            masked[at] = (amplitudes[at].astype(jnp.float32) * kept).astype(masked.dtype)


def read_notes(arrays, notes_wide, notes, sem):
    unit = 0
    for array in arrays:
        _, height, _ = array.shape
        for member in range(array.shape[0]):
            note = array[member, pl.ds(height - NOTE_ROWS, NOTE_ROWS)]
            notes_wide[pl.ds(unit, 1)] = note.astype(jnp.float32).astype(jnp.int32)[:1]
            unit += 1
    copy = pltpu.make_async_copy(notes_wide, notes, sem)
    copy.start()
    return copy


def clear_pairs(pairs):
    pairs[...] = jnp.zeros_like(pairs)


def add_unit(array, member, unit, j, n_rows, cap, rows, amps, notes, pairs, total):
    tile = array.shape[-1]

    def place(k):
        code = notes[unit, k]
        used = code >= 0
        row = jnp.where(used, lax.div(code, rows), 0)
        column = jnp.where(used, lax.rem(code, rows), rows)
        lanes = pl.ds(pl.multiple_of(row * tile, tile), tile)
        return amps[j, pl.ds(0, n_rows), lanes], column

    for k in range(0, cap - 1, 2):
        pair = pairs.at[k // 2]
        pair[pl.ds(0, tile), pl.ds(0, tile)] = array[member, pl.ds(k * tile, tile)]
        pair[pl.ds(tile, tile), pl.ds(tile, tile)] = array[member, pl.ds((k + 1) * tile, tile)]
        (left, first), (right, second) = place(k), place(k + 1)
        both = jnp.dot(
            jnp.concatenate([left, right], axis=1),
            pair[...],
            preferred_element_type=jnp.float32,
        )
        total[first] += both[:, :tile]
        total[second] += both[:, tile:]
    if cap % 2:
        left, column = place(cap - 1)
        total[column] += jnp.dot(
            left,
            array[member, pl.ds((cap - 1) * tile, tile)],
            preferred_element_type=jnp.float32,
        )


def add_arrays(arrays, layout, cap, rows, amps, notes_wide, notes, pairs, total, sem):
    copy = read_notes(arrays, notes_wide, notes, sem)
    pairs[...] = jnp.zeros_like(pairs)
    total[...] = jnp.zeros_like(total)
    copy.wait()
    unit = 0
    for array, partners in zip(arrays, layout):

        def one(i, carry, unit=unit, array=array, partners=partners):
            add_unit(
                array, i, unit + i, partners[0] + i, total.shape[1], cap, rows, amps, notes, pairs, total
            )
            return carry

        lax.fori_loop(0, len(partners), one, 0)
        unit += len(partners)


def first_ladder_kernel(cap, layout, occupied, amps, *refs):
    arrays, (total, occupied_out, notes_wide, notes, pairs, sem) = (
        refs[: len(layout)],
        refs[len(layout) :],
    )
    rows = total.shape[0] - 1
    add_arrays(arrays, layout, cap, rows, amps, notes_wide, notes, pairs, total, sem)
    tile = occupied_out.shape[-1]
    for o in range(occupied.shape[0]):
        wide = jnp.broadcast_to(occupied[pl.ds(o, 1)], (tile, tile))
        occupied_out[pl.ds(o * tile, tile)] = wide.T


def second_ladder_kernel(cap, layout, before, amps, *refs):
    arrays, (own, twin, total, notes_wide, notes, pairs, sem) = (
        refs[: len(layout)],
        refs[len(layout) :],
    )
    rows, n_rows, _ = own.shape
    add_arrays(arrays, layout, cap, rows, amps, notes_wide, notes, pairs, total, sem)
    own[...] = before[:rows, :n_rows] + total[:rows, :n_rows]
    twin[...] = (before[:rows, n_rows:] + total[:rows, n_rows:]).astype(twin.dtype)


def update_kernel(cap, partners, live, amplitudes, driver, own, twin, occupied, virtual, *refs):
    amps, *arrays = refs[: 1 + CORES]
    new, residual, new_buf, residual_buf, notes_wide, notes, pairs, total, sem, sems = refs[
        1 + CORES :
    ]
    rows, _, tile = own.shape
    layout = [partners] * CORES
    add_arrays(arrays, layout, cap, rows, amps, notes_wide, notes, pairs, total, sem)
    copies = []
    for c in range(rows):
        lanes = pl.ds(c * tile, tile)
        for o in range(live.shape[0]):
            here = pl.ds(o * tile, tile)
            at = (here, lanes)
            kept = live[o, c].astype(jnp.float32)
            plain = amplitudes[at].astype(jnp.float32)
            masked = (plain * kept).astype(jnp.bfloat16).astype(jnp.float32)
            denominator = occupied[here, :] - virtual[:, lanes]
            ladder = own[c, here] + twin[c, here].astype(jnp.float32) + total[c, here]
            rest = (driver[at].astype(jnp.float32) + ladder + denominator * plain) * kept
            residual_buf[at] = rest
            new_buf[at] = (masked - rest / denominator).astype(new.dtype)
        for i, (source, target) in enumerate(((new_buf, new), (residual_buf, residual))):
            copies.append(
                pltpu.make_async_copy(source.at[:, lanes], target.at[:, lanes], sems.at[i, c])
            )
            copies[-1].start()
    for copy in copies:
        copy.wait()


def on_device(
    amplitudes,
    tile_live,
    integrals,
    integral_columns,
    driver_terms,
    occupied_energy,
    virtual_energy,
):
    n_rows, width = amplitudes.shape
    rows, slots, tile, _ = integrals.shape
    n_v, n_o = lax.axis_size("vpair"), lax.axis_size("opair")
    n_z = n_o // CORES
    cap = -(-(rows * slots) // n_v)
    height = cap * tile + NOTE_ROWS
    dtype = integrals.dtype
    in_smem = pl.BlockSpec(memory_space=pltpu.SMEM)
    in_vmem = pl.BlockSpec(memory_space=pltpu.VMEM)
    anywhere = pl.BlockSpec(memory_space=pl.ANY)
    in_hbm = pl.BlockSpec(memory_space=pltpu.HBM)

    def after(values, others):
        return lax.optimization_barrier((values, others))[0]

    def params(*buffers):
        size = sum(math.prod(shape) * jnp.dtype(kind).itemsize for shape, kind in buffers)
        return pltpu.CompilerParams(vmem_limit_bytes=size + SPARE_VMEM)

    parcel = (1, height, tile)
    *parcels, masked = pl.pallas_call(
        functools.partial(pack_kernel, n_v, cap),
        out_shape=[jax.ShapeDtypeStruct(parcel, dtype)] * n_v
        + [jax.ShapeDtypeStruct(amplitudes.shape, amplitudes.dtype)],
        in_specs=[in_smem, in_smem, in_vmem, in_vmem],
        out_specs=[in_vmem] * (n_v + 1),
        scratch_shapes=[pltpu.SMEM((n_v * cap,), jnp.int32)] * 2,
        compiler_params=pltpu.CompilerParams(vmem_limit_bytes=ALL_VMEM),
        name="pack",
    )(integral_columns.T, tile_live, integrals, amplitudes)

    def across_v(value, j):
        name = "amplitudes" if value.ndim == 2 else "parcels"
        with jax.named_scope(f"{name}_from_partner_{j}"):
            return lax.ppermute(value, "vpair", [(i, i ^ j) for i in range(n_v)])

    def across_core(value):
        return lax.ppermute(value, "opair", [(i, i ^ 1) for i in range(n_o)])

    def next_on_ring(value, name):
        ring = [*range(0, n_z, 2), *range(n_z - 1 - n_z % 2, 0, -2)]
        pairs = [
            (source * CORES + core, target * CORES + core)
            for source, target in zip(ring, ring[1:] + ring[:1])
            for core in range(CORES)
        ]
        with jax.named_scope(name):
            return lax.ppermute(value, "opair", pairs)

    def join(values):
        return jnp.concatenate(values) if len(values) > 1 else values[0]

    others = list(range(1, n_v))
    groups = {"near": [0], "early": others[: n_v // 2 - 1], "late": others[n_v // 2 - 1 :]}
    arrived = {0: parcels[0]} | {j: across_v(parcels[j], j) for j in others}
    hops = {name: [join([arrived[j] for j in groups[name]])] for name in groups}
    for name in ("near", "early"):
        hops[name].append(next_on_ring(hops[name][0], f"{name}_hop_1"))
    hops["late"][0] = after(hops["late"][0], (hops["near"][1], hops["early"][0]))
    groups["first"] = groups["near"] + groups["early"]
    hops["late"].append(next_on_ring(hops["late"][0], "late_hop_1"))
    hops["first"] = [None, join([hops["near"][1], hops["early"][1]])]
    for hop in range(2, n_z):
        for name in ("first", "late"):
            hops[name].append(next_on_ring(hops[name][-1], f"{name}_hop_{hop}"))

    a_parts = {0: masked}
    with jax.named_scope("twin_amplitudes_0"):
        a_twins = {0: across_core(masked)}
    ready = after(masked, a_twins[0])
    for j in others:
        a_parts[j] = across_v(ready, j)
    for j in others:
        with jax.named_scope(f"twin_amplitudes_{j}"):
            a_twins[j] = across_core(after(a_parts[j], hops["first"][2]))
    amps = jnp.stack([jnp.concatenate([a_parts[j], a_twins[j]]) for j in range(n_v)])

    sums = (rows + 1, CORES * n_rows, tile)
    pairs = (max(cap // 2, 1), 2 * tile, 2 * tile)

    def ladder_call(kernel, found, before, out_shape, extra_scratch, flops, name):
        arrays, layout = [hops[name][hop] for name, hop in found], [groups[name] for name, _ in found]
        n_units = sum(len(partners) for partners in layout)
        return pl.pallas_call(
            functools.partial(kernel, cap, layout),
            out_shape=out_shape,
            in_specs=[in_vmem] * (2 + len(arrays)),
            out_specs=[in_vmem] * len(out_shape),
            scratch_shapes=extra_scratch
            + [
                pltpu.VMEM((n_units, tile), jnp.int32),
                pltpu.SMEM((n_units, tile), jnp.int32),
                pltpu.VMEM(pairs, dtype),
                pltpu.SemaphoreType.DMA,
            ],
            compiler_params=params(
                ((n_units, height, tile), dtype),
                (sums, jnp.float32),
                (sums, jnp.float32),
                (sums, jnp.float32),
                (amps.shape, dtype),
            ),
            cost_estimate=pl.CostEstimate(
                flops=flops,
                bytes_accessed=1024 * 1024,
                transcendentals=0,
            ),
            name=name,
        )(before, amps, *arrays)

    tail = [("late", n_z - 2), ("first", n_z - 1)]
    head = [("near", 0), ("early", 0), ("late", 0)]
    head += [("first", hop) for hop in range(1, n_z - 1)]
    head += [("late", hop) for hop in range(1, n_z - 2)]
    total, occupied = ladder_call(
        first_ladder_kernel,
        head,
        occupied_energy.reshape(-1, tile),
        [
            jax.ShapeDtypeStruct(sums, jnp.float32),
            jax.ShapeDtypeStruct((n_rows, tile), jnp.float32),
        ],
        [],
        FIRST_FLOPS,
        "ladder_first",
    )
    own, twin = ladder_call(
        second_ladder_kernel,
        tail,
        total,
        [
            jax.ShapeDtypeStruct((rows, n_rows, tile), jnp.float32),
            jax.ShapeDtypeStruct((rows, n_rows, tile), jnp.bfloat16),
        ],
        [pltpu.VMEM(sums, jnp.float32)],
        SECOND_FLOPS,
        "ladder_second",
    )
    last, behind = after(hops["late"][-1], twin), groups["late"]
    twin = across_core(twin)

    n_last = CORES * len(behind)
    sums = (rows + 1, n_rows, tile)
    return pl.pallas_call(
        functools.partial(update_kernel, cap, behind),
        out_shape=[
            jax.ShapeDtypeStruct((n_rows, width), jnp.bfloat16),
            jax.ShapeDtypeStruct((n_rows, width), jnp.float32),
        ],
        in_specs=[in_smem] + [in_vmem] * (7 + CORES),
        out_specs=[in_hbm] * 2,
        scratch_shapes=[
            pltpu.VMEM((n_rows, width), jnp.bfloat16),
            pltpu.VMEM((n_rows, width), jnp.float32),
            pltpu.VMEM((n_last, tile), jnp.int32),
            pltpu.SMEM((n_last, tile), jnp.int32),
            pltpu.VMEM(pairs, dtype),
            pltpu.VMEM(sums, jnp.float32),
            pltpu.SemaphoreType.DMA,
            pltpu.SemaphoreType.DMA((2, rows)),
        ],
        compiler_params=params(
            (amps.shape, dtype), ((n_last, height, tile), dtype), *[(sums, jnp.float32)] * 5
        ),
        name="update",
    )(
        tile_live,
        amplitudes,
        driver_terms,
        own,
        twin,
        occupied,
        virtual_energy.reshape(1, width),
        amps,
        last,
        across_core(last),
    )


def solution(mesh):
    in_specs = (
        P("opair", "vpair"),
        P("opair", "vpair"),
        P("vpair", "opair", None, None),
        P("vpair", "opair"),
        P("opair", "vpair"),
        P("opair"),
        P("vpair"),
    )
    out_specs = (P("opair", "vpair"), P("opair", "vpair"))
    return jax.shard_map(
        on_device, mesh=mesh, in_specs=in_specs, out_specs=out_specs, check_vma=False
    )
```

```python
import functools
import math

import jax
import jax.numpy as jnp
from jax import lax
from jax.experimental import pallas as pl
from jax.experimental.pallas import tpu as pltpu
from jax.sharding import PartitionSpec as P

SPARE_VMEM = 4 * 1024 * 1024
ALL_VMEM = 60 * 1024 * 1024
CORES = 2
NOTE_ROWS = 16
FIRST_FLOPS = 10**8
SECOND_FLOPS = 10**9


def pack_kernel(n_v, cap, columns, live, integrals, amplitudes, *refs):
    parcels, (masked, origin, codes) = refs[:n_v], refs[n_v:]
    rows, slots, tile, _ = integrals.shape
    me = lax.axis_index("vpair")
    counts = [jnp.int32(0)] * n_v
    for i in range(n_v * cap):
        origin[i] = 0
        codes[i] = -1
    for row in range(rows):
        for slot in range(slots):
            column = columns[slot, row]
            partner = lax.div(column, rows) ^ me
            place = counts[0]
            for j in range(1, n_v):
                place = jnp.where(partner == j, counts[j], place)
            counts = [counts[j] + (partner == j).astype(jnp.int32) for j in range(n_v)]
            at = partner * cap + place
            origin[at] = row * slots + slot
            codes[at] = row * rows + lax.rem(column, rows)
    lane = lax.broadcasted_iota(jnp.int32, (NOTE_ROWS, tile), 1)
    for j in range(n_v):
        note = jnp.full((NOTE_ROWS, tile), -1, jnp.int32)
        for k in range(cap):
            entry = origin[j * cap + k]
            parcels[j][0, pl.ds(k * tile, tile)] = integrals[
                lax.div(entry, slots), lax.rem(entry, slots)
            ]
            note = jnp.where(lane == k, codes[j * cap + k], note)
        parcels[j][0, pl.ds(cap * tile, NOTE_ROWS)] = note.astype(jnp.float32).astype(
            integrals.dtype
        )
    for o in range(live.shape[0]):
        for c in range(live.shape[1]):
            at = (pl.ds(o * tile, tile), pl.ds(c * tile, tile))
            kept = live[o, c].astype(jnp.float32)
            masked[at] = (amplitudes[at].astype(jnp.float32) * kept).astype(masked.dtype)


def read_notes(arrays, notes_wide, notes, sem):
    unit = 0
    for array in arrays:
        _, height, _ = array.shape
        for member in range(array.shape[0]):
            note = array[member, pl.ds(height - NOTE_ROWS, NOTE_ROWS)]
            notes_wide[pl.ds(unit, 1)] = note.astype(jnp.float32).astype(jnp.int32)[:1]
            unit += 1
    copy = pltpu.make_async_copy(notes_wide, notes, sem)
    copy.start()
    return copy


def clear_pairs(pairs):
    pairs[...] = jnp.zeros_like(pairs)


def add_unit(array, member, unit, j, n_rows, cap, rows, amps, notes, pairs, total):
    tile = array.shape[-1]

    def place(k):
        code = notes[unit, k]
        used = code >= 0
        row = jnp.where(used, lax.div(code, rows), 0)
        column = jnp.where(used, lax.rem(code, rows), rows)
        lanes = pl.ds(pl.multiple_of(row * tile, tile), tile)
        return amps[j, pl.ds(0, n_rows), lanes], column

    for k in range(0, cap - 1, 2):
        pair = pairs.at[k // 2]
        pair[pl.ds(0, tile), pl.ds(0, tile)] = array[member, pl.ds(k * tile, tile)]
        pair[pl.ds(tile, tile), pl.ds(tile, tile)] = array[member, pl.ds((k + 1) * tile, tile)]
        (left, first), (right, second) = place(k), place(k + 1)
        both = jnp.dot(
            jnp.concatenate([left, right], axis=1),
            pair[...],
            preferred_element_type=jnp.float32,
        )
        total[first] += both[:, :tile]
        total[second] += both[:, tile:]
    if cap % 2:
        left, column = place(cap - 1)
        total[column] += jnp.dot(
            left,
            array[member, pl.ds((cap - 1) * tile, tile)],
            preferred_element_type=jnp.float32,
        )


def add_arrays(arrays, layout, cap, rows, amps, notes_wide, notes, pairs, total, sem):
    copy = read_notes(arrays, notes_wide, notes, sem)
    pairs[...] = jnp.zeros_like(pairs)
    total[...] = jnp.zeros_like(total)
    copy.wait()
    unit = 0
    for array, partners in zip(arrays, layout):

        def one(i, carry, unit=unit, array=array, partners=partners):
            add_unit(
                array, i, unit + i, partners[0] + i, total.shape[1], cap, rows, amps, notes, pairs, total
            )
            return carry

        lax.fori_loop(0, len(partners), one, 0)
        unit += len(partners)


def first_ladder_kernel(cap, layout, occupied, amps, *refs):
    arrays, (total, occupied_out, notes_wide, notes, pairs, sem) = (
        refs[: len(layout)],
        refs[len(layout) :],
    )
    rows = total.shape[0] - 1
    add_arrays(arrays, layout, cap, rows, amps, notes_wide, notes, pairs, total, sem)
    tile = occupied_out.shape[-1]
    for o in range(occupied.shape[0]):
        wide = jnp.broadcast_to(occupied[pl.ds(o, 1)], (tile, tile))
        occupied_out[pl.ds(o * tile, tile)] = wide.T


def second_ladder_kernel(cap, layout, before, amps, *refs):
    arrays, (own, twin, total, notes_wide, notes, pairs, sem) = (
        refs[: len(layout)],
        refs[len(layout) :],
    )
    rows, n_rows, _ = own.shape
    add_arrays(arrays, layout, cap, rows, amps, notes_wide, notes, pairs, total, sem)
    own[...] = before[:rows, :n_rows] + total[:rows, :n_rows]
    twin[...] = (before[:rows, n_rows:] + total[:rows, n_rows:]).astype(twin.dtype)


def update_kernel(cap, partners, live, amplitudes, driver, own, twin, occupied, virtual, *refs):
    amps, *arrays = refs[: 1 + CORES]
    new, residual, new_buf, residual_buf, notes_wide, notes, pairs, total, sem, sems = refs[
        1 + CORES :
    ]
    rows, _, tile = own.shape
    layout = [partners] * CORES
    add_arrays(arrays, layout, cap, rows, amps, notes_wide, notes, pairs, total, sem)
    copies = []
    for c in range(rows):
        lanes = pl.ds(c * tile, tile)
        for o in range(live.shape[0]):
            here = pl.ds(o * tile, tile)
            at = (here, lanes)
            kept = live[o, c].astype(jnp.float32)
            plain = amplitudes[at].astype(jnp.float32)
            masked = (plain * kept).astype(jnp.bfloat16).astype(jnp.float32)
            denominator = occupied[here, :] - virtual[:, lanes]
            ladder = own[c, here] + twin[c, here].astype(jnp.float32) + total[c, here]
            rest = (driver[at].astype(jnp.float32) + ladder + denominator * plain) * kept
            residual_buf[at] = rest
            new_buf[at] = (masked - rest / denominator).astype(new.dtype)
        for i, (source, target) in enumerate(((new_buf, new), (residual_buf, residual))):
            copies.append(
                pltpu.make_async_copy(source.at[:, lanes], target.at[:, lanes], sems.at[i, c])
            )
            copies[-1].start()
    for copy in copies:
        copy.wait()


def on_device(
    amplitudes,
    tile_live,
    integrals,
    integral_columns,
    driver_terms,
    occupied_energy,
    virtual_energy,
):
    n_rows, width = amplitudes.shape
    rows, slots, tile, _ = integrals.shape
    n_v, n_o = lax.axis_size("vpair"), lax.axis_size("opair")
    n_z = n_o // CORES
    cap = -(-(rows * slots) // n_v)
    height = cap * tile + NOTE_ROWS
    dtype = integrals.dtype
    in_smem = pl.BlockSpec(memory_space=pltpu.SMEM)
    in_vmem = pl.BlockSpec(memory_space=pltpu.VMEM)
    anywhere = pl.BlockSpec(memory_space=pl.ANY)
    in_hbm = pl.BlockSpec(memory_space=pltpu.HBM)

    def after(values, others):
        return lax.optimization_barrier((values, others))[0]

    def params(*buffers):
        size = sum(math.prod(shape) * jnp.dtype(kind).itemsize for shape, kind in buffers)
        return pltpu.CompilerParams(vmem_limit_bytes=size + SPARE_VMEM)

    parcel = (1, height, tile)
    *parcels, masked = pl.pallas_call(
        functools.partial(pack_kernel, n_v, cap),
        out_shape=[jax.ShapeDtypeStruct(parcel, dtype)] * n_v
        + [jax.ShapeDtypeStruct(amplitudes.shape, amplitudes.dtype)],
        in_specs=[in_smem, in_smem, in_vmem, in_vmem],
        out_specs=[in_vmem] * (n_v + 1),
        scratch_shapes=[pltpu.SMEM((n_v * cap,), jnp.int32)] * 2,
        compiler_params=pltpu.CompilerParams(vmem_limit_bytes=ALL_VMEM),
        name="pack",
    )(integral_columns.T, tile_live, integrals, amplitudes)

    def across_v(value, j):
        name = "amplitudes" if value.ndim == 2 else "parcels"
        with jax.named_scope(f"{name}_from_partner_{j}"):
            return lax.ppermute(value, "vpair", [(i, i ^ j) for i in range(n_v)])

    def across_core(value):
        return lax.ppermute(value, "opair", [(i, i ^ 1) for i in range(n_o)])

    def next_on_ring(value, name):
        ring = [*range(0, n_z, 2), *range(n_z - 1 - n_z % 2, 0, -2)]
        pairs = [
            (source * CORES + core, target * CORES + core)
            for source, target in zip(ring, ring[1:] + ring[:1])
            for core in range(CORES)
        ]
        with jax.named_scope(name):
            return lax.ppermute(value, "opair", pairs)

    def join(values):
        return jnp.concatenate(values) if len(values) > 1 else values[0]

    others = list(range(1, n_v))
    groups = {"near": [0], "early": others[: n_v // 2 - 1], "late": others[n_v // 2 - 1 :]}
    arrived = {0: parcels[0]} | {j: across_v(parcels[j], j) for j in others}
    hops = {name: [join([arrived[j] for j in groups[name]])] for name in groups}
    for name in ("near", "early"):
        hops[name].append(next_on_ring(hops[name][0], f"{name}_hop_1"))
    hops["late"][0] = after(hops["late"][0], (hops["near"][1], hops["early"][0]))
    groups["first"] = groups["near"] + groups["early"]
    hops["late"].append(next_on_ring(hops["late"][0], "late_hop_1"))
    hops["first"] = [None, join([hops["near"][1], hops["early"][1]])]
    for hop in range(2, n_z):
        for name in ("first", "late"):
            hops[name].append(next_on_ring(hops[name][-1], f"{name}_hop_{hop}"))

    def gather_amplitudes(value, bits):
        held, ids = value[None], [0]
        twin_held = None
        for bit in bits:
            with jax.named_scope(f"amplitudes_bit_{bit}"):
                arrived_now = lax.ppermute(held, "vpair", [(i, i ^ bit) for i in range(n_v)])
            with jax.named_scope(f"twin_of_bit_{bit}"):
                part = arrived_now if twin_held is not None else jnp.concatenate([held, arrived_now])
                twin_now = across_core(after(part, hops["late"][1]))
            twin_held = twin_now if twin_held is None else jnp.concatenate([twin_held, twin_now])
            held, ids = jnp.concatenate([held, arrived_now]), ids + [i ^ bit for i in ids]
        return {j: (held[i], twin_held[i]) for i, j in enumerate(ids)}

    bits = [1 << i for i in range((n_v - 1).bit_length())]
    ready = after(masked, (hops["late"][0], hops["early"][1]))
    upper = gather_amplitudes(ready[: n_rows // 2], bits)
    lower = gather_amplitudes(ready[n_rows // 2 :], bits[::-1])
    amps = jnp.stack(
        [
            jnp.concatenate([upper[j][0], lower[j][0], upper[j][1], lower[j][1]])
            for j in range(n_v)
        ]
    )

    sums = (rows + 1, CORES * n_rows, tile)
    pairs = (max(cap // 2, 1), 2 * tile, 2 * tile)

    def ladder_call(kernel, found, before, out_shape, extra_scratch, flops, name):
        arrays, layout = [hops[name][hop] for name, hop in found], [groups[name] for name, _ in found]
        n_units = sum(len(partners) for partners in layout)
        return pl.pallas_call(
            functools.partial(kernel, cap, layout),
            out_shape=out_shape,
            in_specs=[in_vmem] * (2 + len(arrays)),
            out_specs=[in_vmem] * len(out_shape),
            scratch_shapes=extra_scratch
            + [
                pltpu.VMEM((n_units, tile), jnp.int32),
                pltpu.SMEM((n_units, tile), jnp.int32),
                pltpu.VMEM(pairs, dtype),
                pltpu.SemaphoreType.DMA,
            ],
            compiler_params=params(
                ((n_units, height, tile), dtype),
                (sums, jnp.float32),
                (sums, jnp.float32),
                (sums, jnp.float32),
                (amps.shape, dtype),
            ),
            cost_estimate=pl.CostEstimate(
                flops=flops,
                bytes_accessed=1024 * 1024,
                transcendentals=0,
            ),
            name=name,
        )(before, amps, *arrays)

    tail = [("late", n_z - 2), ("first", n_z - 1)]
    head = [("near", 0), ("early", 0), ("late", 0)]
    head += [("first", hop) for hop in range(1, n_z - 1)]
    head += [("late", hop) for hop in range(1, n_z - 2)]
    total, occupied = ladder_call(
        first_ladder_kernel,
        head,
        occupied_energy.reshape(-1, tile),
        [
            jax.ShapeDtypeStruct(sums, jnp.float32),
            jax.ShapeDtypeStruct((n_rows, tile), jnp.float32),
        ],
        [],
        FIRST_FLOPS,
        "ladder_first",
    )
    own, twin = ladder_call(
        second_ladder_kernel,
        tail,
        total,
        [
            jax.ShapeDtypeStruct((rows, n_rows, tile), jnp.float32),
            jax.ShapeDtypeStruct((rows, n_rows, tile), jnp.bfloat16),
        ],
        [pltpu.VMEM(sums, jnp.float32)],
        SECOND_FLOPS,
        "ladder_second",
    )
    last, behind = after(hops["late"][-1], twin), groups["late"]
    twin = across_core(twin)

    n_last = CORES * len(behind)
    sums = (rows + 1, n_rows, tile)
    return pl.pallas_call(
        functools.partial(update_kernel, cap, behind),
        out_shape=[
            jax.ShapeDtypeStruct((n_rows, width), jnp.bfloat16),
            jax.ShapeDtypeStruct((n_rows, width), jnp.float32),
        ],
        in_specs=[in_smem] + [in_vmem] * (7 + CORES),
        out_specs=[in_hbm] * 2,
        scratch_shapes=[
            pltpu.VMEM((n_rows, width), jnp.bfloat16),
            pltpu.VMEM((n_rows, width), jnp.float32),
            pltpu.VMEM((n_last, tile), jnp.int32),
            pltpu.SMEM((n_last, tile), jnp.int32),
            pltpu.VMEM(pairs, dtype),
            pltpu.VMEM(sums, jnp.float32),
            pltpu.SemaphoreType.DMA,
            pltpu.SemaphoreType.DMA((2, rows)),
        ],
        compiler_params=params(
            (amps.shape, dtype), ((n_last, height, tile), dtype), *[(sums, jnp.float32)] * 5
        ),
        name="update",
    )(
        tile_live,
        amplitudes,
        driver_terms,
        own,
        twin,
        occupied,
        virtual_energy.reshape(1, width),
        amps,
        last,
        across_core(last),
    )


def solution(mesh):
    in_specs = (
        P("opair", "vpair"),
        P("opair", "vpair"),
        P("vpair", "opair", None, None),
        P("vpair", "opair"),
        P("opair", "vpair"),
        P("opair"),
        P("vpair"),
    )
    out_specs = (P("opair", "vpair"), P("opair", "vpair"))
    return jax.shard_map(
        on_device, mesh=mesh, in_specs=in_specs, out_specs=out_specs, check_vma=False
    )
```

```python
import functools
import math

import jax
import jax.numpy as jnp
from jax import lax
from jax.experimental import pallas as pl
from jax.experimental.pallas import tpu as pltpu
from jax.sharding import PartitionSpec as P

SPARE_VMEM = 4 * 1024 * 1024
ALL_VMEM = 60 * 1024 * 1024
CORES = 2
NOTE_ROWS = 16
FIRST_FLOPS = 10**8
SECOND_FLOPS = 10**9


def pack_kernel(n_v, cap, columns, live, integrals, amplitudes, *refs):
    parcels, halves, refs = refs[:n_v], refs[n_v : n_v + 2], refs[n_v + 2 :]
    origin, codes, tiles, plain, boxes, masked, in_sems, out_sems = refs
    rows, slots, tile, _ = integrals.shape
    me = lax.axis_index("vpair")
    copies_in = [
        pltpu.make_async_copy(integrals, tiles, in_sems.at[0]),
        pltpu.make_async_copy(amplitudes, plain, in_sems.at[1]),
    ]
    copies_out = [pltpu.make_async_copy(boxes.at[j], parcels[j], out_sems.at[j]) for j in range(n_v)]
    copies_out += [
        pltpu.make_async_copy(masked.at[i], halves[i], out_sems.at[n_v + i]) for i in range(2)
    ]
    for copy in copies_in:
        copy.start()
    counts = [jnp.int32(0)] * n_v
    for i in range(n_v * cap):
        origin[i] = 0
        codes[i] = -1
    for row in range(rows):
        for slot in range(slots):
            column = columns[slot, row]
            partner = lax.div(column, rows) ^ me
            place = counts[0]
            for j in range(1, n_v):
                place = jnp.where(partner == j, counts[j], place)
            counts = [counts[j] + (partner == j).astype(jnp.int32) for j in range(n_v)]
            at = partner * cap + place
            origin[at] = row * slots + slot
            codes[at] = row * rows + lax.rem(column, rows)
    copies_in[0].wait()
    lane = lax.broadcasted_iota(jnp.int32, (NOTE_ROWS, tile), 1)
    for j in range(n_v):
        note = jnp.full((NOTE_ROWS, tile), -1, jnp.int32)
        for k in range(cap):
            entry = origin[j * cap + k]
            boxes[j, 0, pl.ds(k * tile, tile)] = tiles[
                lax.div(entry, slots), lax.rem(entry, slots)
            ]
            note = jnp.where(lane == k, codes[j * cap + k], note)
        boxes[j, 0, pl.ds(cap * tile, NOTE_ROWS)] = note.astype(jnp.float32).astype(boxes.dtype)
        copies_out[j].start()
    copies_in[1].wait()
    half_rows = masked.shape[1]
    for o in range(live.shape[0]):
        for c in range(live.shape[1]):
            lanes = pl.ds(c * tile, tile)
            kept = live[o, c].astype(jnp.float32)
            value = (plain[pl.ds(o * tile, tile), lanes].astype(jnp.float32) * kept).astype(
                masked.dtype
            )
            for first in range(o * tile, (o + 1) * tile, half_rows):
                rows_here = min(half_rows, tile)
                masked[first // half_rows, pl.ds(first % half_rows, rows_here), lanes] = value[
                    first - o * tile : first - o * tile + rows_here
                ]
    for copy in copies_out[n_v:]:
        copy.start()
    for copy in copies_out:
        copy.wait()


def read_notes(arrays, notes_wide, notes, sem):
    unit = 0
    for array in arrays:
        _, height, _ = array.shape
        for member in range(array.shape[0]):
            note = array[member, pl.ds(height - NOTE_ROWS, NOTE_ROWS)]
            notes_wide[pl.ds(unit, 1)] = note.astype(jnp.float32).astype(jnp.int32)[:1]
            unit += 1
    copy = pltpu.make_async_copy(notes_wide, notes, sem)
    copy.start()
    return copy


def clear_pairs(pairs):
    pairs[...] = jnp.zeros_like(pairs)


def add_unit(array, member, unit, j, n_rows, cap, rows, amps, notes, pairs, total):
    tile = array.shape[-1]

    def place(k):
        code = notes[unit, k]
        used = code >= 0
        row = jnp.where(used, lax.div(code, rows), 0)
        column = jnp.where(used, lax.rem(code, rows), rows)
        lanes = pl.ds(pl.multiple_of(row * tile, tile), tile)
        return amps[j, pl.ds(0, n_rows), lanes], column

    for k in range(0, cap - 1, 2):
        pair = pairs.at[k // 2]
        pair[pl.ds(0, tile), pl.ds(0, tile)] = array[member, pl.ds(k * tile, tile)]
        pair[pl.ds(tile, tile), pl.ds(tile, tile)] = array[member, pl.ds((k + 1) * tile, tile)]
        (left, first), (right, second) = place(k), place(k + 1)
        both = jnp.dot(
            jnp.concatenate([left, right], axis=1),
            pair[...],
            preferred_element_type=jnp.float32,
        )
        total[first] += both[:, :tile]
        total[second] += both[:, tile:]
    if cap % 2:
        left, column = place(cap - 1)
        total[column] += jnp.dot(
            left,
            array[member, pl.ds((cap - 1) * tile, tile)],
            preferred_element_type=jnp.float32,
        )


def add_arrays(arrays, layout, cap, rows, amps, notes_wide, notes, pairs, total, sem):
    copy = read_notes(arrays, notes_wide, notes, sem)
    pairs[...] = jnp.zeros_like(pairs)
    total[...] = jnp.zeros_like(total)
    copy.wait()
    unit = 0
    for array, partners in zip(arrays, layout):

        def one(i, carry, unit=unit, array=array, partners=partners):
            add_unit(
                array, i, unit + i, partners[0] + i, total.shape[1], cap, rows, amps, notes, pairs, total
            )
            return carry

        lax.fori_loop(0, len(partners), one, 0)
        unit += len(partners)


def first_ladder_kernel(cap, layout, occupied, virtual, amps, *refs):
    arrays, (total, occupied_out, inverse, notes_wide, notes, pairs, sem) = (
        refs[: len(layout)],
        refs[len(layout) :],
    )
    rows = total.shape[0] - 1
    add_arrays(arrays, layout, cap, rows, amps, notes_wide, notes, pairs, total, sem)
    tile = occupied_out.shape[-1]
    for o in range(occupied.shape[0]):
        here = pl.ds(o * tile, tile)
        column = jnp.broadcast_to(occupied[pl.ds(o, 1)], (tile, tile)).T
        occupied_out[here] = column
        for c in range(rows):
            lanes = pl.ds(c * tile, tile)
            inverse[here, lanes] = 1.0 / (column - virtual[:, lanes])


def second_ladder_kernel(
    cap, layout, before, driver, amplitudes, occupied, virtual, amps, *refs
):
    arrays, (base, twin, total, notes_wide, notes, pairs, sem) = (
        refs[: len(layout)],
        refs[len(layout) :],
    )
    rows, n_rows, tile = twin.shape
    add_arrays(arrays, layout, cap, rows, amps, notes_wide, notes, pairs, total, sem)
    twin[...] = (before[:rows, n_rows:] + total[:rows, n_rows:]).astype(twin.dtype)
    for c in range(rows):
        lanes = pl.ds(c * tile, tile)
        own = before[c, :n_rows] + total[c, :n_rows]
        denominator = occupied[...] - virtual[:, lanes]
        plain = amplitudes[:, lanes].astype(jnp.float32)
        base[:, lanes] = driver[:, lanes].astype(jnp.float32) + own + denominator * plain


def update_kernel(cap, partners, live, amplitudes, base, inverse, twin, *refs):
    amps, *arrays = refs[: 1 + CORES]
    new, residual, new_buf, residual_buf, notes_wide, notes, pairs, total, sem, sems = refs[
        1 + CORES :
    ]
    rows, _, tile = twin.shape
    layout = [partners] * CORES
    add_arrays(arrays, layout, cap, rows, amps, notes_wide, notes, pairs, total, sem)
    copies = []
    for c in range(rows):
        lanes = pl.ds(c * tile, tile)
        for o in range(live.shape[0]):
            here = pl.ds(o * tile, tile)
            at = (here, lanes)
            kept = live[o, c].astype(jnp.float32)
            masked = (amplitudes[at].astype(jnp.float32) * kept).astype(jnp.bfloat16)
            rest = (base[at] + (twin[c, here].astype(jnp.float32) + total[c, here])) * kept
            residual_buf[at] = rest
            new_buf[at] = (masked.astype(jnp.float32) - rest * inverse[at]).astype(new.dtype)
        for i, (source, target) in enumerate(((new_buf, new), (residual_buf, residual))):
            copies.append(
                pltpu.make_async_copy(source.at[:, lanes], target.at[:, lanes], sems.at[i, c])
            )
            copies[-1].start()
    for copy in copies:
        copy.wait()


def on_device(
    amplitudes,
    tile_live,
    integrals,
    integral_columns,
    driver_terms,
    occupied_energy,
    virtual_energy,
):
    n_rows, width = amplitudes.shape
    rows, slots, tile, _ = integrals.shape
    n_v, n_o = lax.axis_size("vpair"), lax.axis_size("opair")
    n_z = n_o // CORES
    cap = -(-(rows * slots) // n_v)
    height = cap * tile + NOTE_ROWS
    dtype = integrals.dtype
    in_smem = pl.BlockSpec(memory_space=pltpu.SMEM)
    in_vmem = pl.BlockSpec(memory_space=pltpu.VMEM)
    anywhere = pl.BlockSpec(memory_space=pl.ANY)
    in_hbm = pl.BlockSpec(memory_space=pltpu.HBM)

    def after(values, others):
        return lax.optimization_barrier((values, others))[0]

    def params(*buffers):
        size = sum(math.prod(shape) * jnp.dtype(kind).itemsize for shape, kind in buffers)
        return pltpu.CompilerParams(vmem_limit_bytes=size + SPARE_VMEM)

    parcel = (1, height, tile)
    half = (n_rows // 2, width)
    *parcels, upper, lower = pl.pallas_call(
        functools.partial(pack_kernel, n_v, cap),
        out_shape=[jax.ShapeDtypeStruct(parcel, dtype)] * n_v
        + [jax.ShapeDtypeStruct(half, amplitudes.dtype)] * 2,
        in_specs=[in_smem, in_smem, in_hbm, in_hbm],
        out_specs=[in_hbm] * (n_v + 2),
        scratch_shapes=[pltpu.SMEM((n_v * cap,), jnp.int32)] * 2
        + [
            pltpu.VMEM(integrals.shape, dtype),
            pltpu.VMEM(amplitudes.shape, amplitudes.dtype),
            pltpu.VMEM((n_v, *parcel), dtype),
            pltpu.VMEM((2, *half), amplitudes.dtype),
            pltpu.SemaphoreType.DMA((2,)),
            pltpu.SemaphoreType.DMA((n_v + 2,)),
        ],
        compiler_params=pltpu.CompilerParams(vmem_limit_bytes=ALL_VMEM),
        name="pack",
    )(integral_columns.T, tile_live, integrals, amplitudes)

    def across_v(value, j):
        name = "amplitudes" if value.ndim == 2 else "parcels"
        with jax.named_scope(f"{name}_from_partner_{j}"):
            return lax.ppermute(value, "vpair", [(i, i ^ j) for i in range(n_v)])

    def across_core(value):
        return lax.ppermute(value, "opair", [(i, i ^ 1) for i in range(n_o)])

    def next_on_ring(value, name):
        ring = [*range(0, n_z, 2), *range(n_z - 1 - n_z % 2, 0, -2)]
        pairs = [
            (source * CORES + core, target * CORES + core)
            for source, target in zip(ring, ring[1:] + ring[:1])
            for core in range(CORES)
        ]
        with jax.named_scope(name):
            return lax.ppermute(value, "opair", pairs)

    def join(values):
        return jnp.concatenate(values) if len(values) > 1 else values[0]

    others = list(range(1, n_v))
    groups = {"near": [0], "early": others[: n_v // 2 - 1], "late": others[n_v // 2 - 1 :]}
    arrived = {0: parcels[0]} | {j: across_v(parcels[j], j) for j in others}
    hops = {name: [join([arrived[j] for j in groups[name]])] for name in groups}
    hops["near"].append(next_on_ring(hops["near"][0], "near_hop_1"))
    hops["early"][0] = after(hops["early"][0], hops["near"][1])
    hops["early"].append(next_on_ring(hops["early"][0], "early_hop_1"))
    hops["late"][0] = after(hops["late"][0], (hops["near"][1], hops["early"][0]))
    groups["first"] = groups["near"] + groups["early"]
    hops["late"].append(next_on_ring(hops["late"][0], "late_hop_1"))
    hops["first"] = [None, join([hops["near"][1], hops["early"][1]])]
    for hop in range(2, n_z):
        for name in ("first", "late"):
            hops[name].append(next_on_ring(hops[name][-1], f"{name}_hop_{hop}"))

    def gather_amplitudes(value, bits):
        held, ids = value[None], [0]
        twin_held = None
        for bit in bits:
            with jax.named_scope(f"amplitudes_bit_{bit}"):
                arrived_now = lax.ppermute(held, "vpair", [(i, i ^ bit) for i in range(n_v)])
            with jax.named_scope(f"twin_of_bit_{bit}"):
                part = arrived_now if twin_held is not None else jnp.concatenate([held, arrived_now])
                twin_now = across_core(after(part, hops["late"][1]))
            twin_held = twin_now if twin_held is None else jnp.concatenate([twin_held, twin_now])
            held, ids = jnp.concatenate([held, arrived_now]), ids + [i ^ bit for i in ids]
        return {j: (held[i], twin_held[i]) for i, j in enumerate(ids)}

    bits = [1 << i for i in range((n_v - 1).bit_length())]
    upper, lower = after((upper, lower), (hops["late"][0], hops["early"][1]))
    upper, lower = gather_amplitudes(upper, bits), gather_amplitudes(lower, bits[::-1])
    amps = jnp.stack(
        [
            jnp.concatenate([upper[j][0], lower[j][0], upper[j][1], lower[j][1]])
            for j in range(n_v)
        ]
    )

    sums = (rows + 1, CORES * n_rows, tile)
    pairs = (max(cap // 2, 1), 2 * tile, 2 * tile)

    def ladder_call(kernel, found, before, out_shape, extra_scratch, flops, name):
        arrays, layout = [hops[name][hop] for name, hop in found], [groups[name] for name, _ in found]
        n_units = sum(len(partners) for partners in layout)
        return pl.pallas_call(
            functools.partial(kernel, cap, layout),
            out_shape=out_shape,
            in_specs=[in_vmem] * (len(before) + 1 + len(arrays)),
            out_specs=[in_vmem] * len(out_shape),
            scratch_shapes=extra_scratch
            + [
                pltpu.VMEM((n_units, tile), jnp.int32),
                pltpu.SMEM((n_units, tile), jnp.int32),
                pltpu.VMEM(pairs, dtype),
                pltpu.SemaphoreType.DMA,
            ],
            compiler_params=params(
                ((n_units, height, tile), dtype),
                *[(sums, jnp.float32)] * 4,
                (amps.shape, dtype),
            ),
            cost_estimate=pl.CostEstimate(
                flops=flops,
                bytes_accessed=1024 * 1024,
                transcendentals=0,
            ),
            name=name,
        )(*before, amps, *arrays)

    tail = [("late", n_z - 2), ("first", n_z - 1)]
    head = [("near", 0), ("early", 0), ("late", 0)]
    head += [("first", hop) for hop in range(1, n_z - 1)]
    head += [("late", hop) for hop in range(1, n_z - 2)]
    virtual = virtual_energy.reshape(1, width)
    total, occupied, inverse = ladder_call(
        first_ladder_kernel,
        head,
        [occupied_energy.reshape(-1, tile), virtual],
        [
            jax.ShapeDtypeStruct(sums, jnp.float32),
            jax.ShapeDtypeStruct((n_rows, tile), jnp.float32),
            jax.ShapeDtypeStruct((n_rows, width), jnp.float32),
        ],
        [],
        FIRST_FLOPS,
        "ladder_first",
    )
    base, twin = ladder_call(
        second_ladder_kernel,
        tail,
        [total, driver_terms, amplitudes, occupied, virtual],
        [
            jax.ShapeDtypeStruct((n_rows, width), jnp.float32),
            jax.ShapeDtypeStruct((rows, n_rows, tile), jnp.bfloat16),
        ],
        [pltpu.VMEM(sums, jnp.float32)],
        SECOND_FLOPS,
        "ladder_second",
    )
    last, behind = after(hops["late"][-1], twin), groups["late"]
    twin = across_core(twin)

    n_last = CORES * len(behind)
    sums = (rows + 1, n_rows, tile)
    return pl.pallas_call(
        functools.partial(update_kernel, cap, behind),
        out_shape=[
            jax.ShapeDtypeStruct((n_rows, width), jnp.bfloat16),
            jax.ShapeDtypeStruct((n_rows, width), jnp.float32),
        ],
        in_specs=[in_smem] + [in_vmem] * (5 + CORES),
        out_specs=[in_hbm] * 2,
        scratch_shapes=[
            pltpu.VMEM((n_rows, width), jnp.bfloat16),
            pltpu.VMEM((n_rows, width), jnp.float32),
            pltpu.VMEM((n_last, tile), jnp.int32),
            pltpu.SMEM((n_last, tile), jnp.int32),
            pltpu.VMEM(pairs, dtype),
            pltpu.VMEM(sums, jnp.float32),
            pltpu.SemaphoreType.DMA,
            pltpu.SemaphoreType.DMA((2, rows)),
        ],
        compiler_params=params(
            (amps.shape, dtype), ((n_last, height, tile), dtype), *[(sums, jnp.float32)] * 5
        ),
        name="update",
    )(
        tile_live,
        amplitudes,
        base,
        inverse,
        twin,
        amps,
        last,
        across_core(last),
    )


def solution(mesh):
    in_specs = (
        P("opair", "vpair"),
        P("opair", "vpair"),
        P("vpair", "opair", None, None),
        P("vpair", "opair"),
        P("opair", "vpair"),
        P("opair"),
        P("vpair"),
    )
    out_specs = (P("opair", "vpair"), P("opair", "vpair"))
    return jax.shard_map(
        on_device, mesh=mesh, in_specs=in_specs, out_specs=out_specs, check_vma=False
    )
```

```python
import functools
import math

import jax
import jax.numpy as jnp
from jax import lax
from jax.experimental import pallas as pl
from jax.experimental.pallas import tpu as pltpu
from jax.sharding import PartitionSpec as P

SPARE_VMEM = 4 * 1024 * 1024
ALL_VMEM = 60 * 1024 * 1024
CORES = 2
NOTE_ROWS = 16
FIRST_FLOPS = 10**9
MIDDLE_FLOPS = 10**8
LAST_FLOPS = 10**9


def pack_kernel(n_v, cap, columns, live, integrals, amplitudes, *refs):
    parcels, halves, refs = refs[:n_v], refs[n_v : n_v + 2], refs[n_v + 2 :]
    origin, codes, tiles, plain, boxes, masked, in_sems, out_sems = refs
    rows, slots, tile, _ = integrals.shape
    me = lax.axis_index("vpair")
    copies_in = [
        pltpu.make_async_copy(integrals, tiles, in_sems.at[0]),
        pltpu.make_async_copy(amplitudes, plain, in_sems.at[1]),
    ]
    copies_out = [pltpu.make_async_copy(boxes.at[j], parcels[j], out_sems.at[j]) for j in range(n_v)]
    copies_out += [
        pltpu.make_async_copy(masked.at[i], halves[i], out_sems.at[n_v + i]) for i in range(2)
    ]
    for copy in copies_in:
        copy.start()
    counts = [jnp.int32(0)] * n_v
    for i in range(n_v * cap):
        origin[i] = 0
        codes[i] = -1
    for row in range(rows):
        for slot in range(slots):
            column = columns[slot, row]
            partner = lax.div(column, rows) ^ me
            place = counts[0]
            for j in range(1, n_v):
                place = jnp.where(partner == j, counts[j], place)
            counts = [counts[j] + (partner == j).astype(jnp.int32) for j in range(n_v)]
            at = partner * cap + place
            origin[at] = row * slots + slot
            codes[at] = row * rows + lax.rem(column, rows)
    copies_in[0].wait()
    lane = lax.broadcasted_iota(jnp.int32, (NOTE_ROWS, tile), 1)
    for j in range(n_v):
        note = jnp.full((NOTE_ROWS, tile), -1, jnp.int32)
        for k in range(cap):
            entry = origin[j * cap + k]
            boxes[j, 0, pl.ds(k * tile, tile)] = tiles[
                lax.div(entry, slots), lax.rem(entry, slots)
            ]
            note = jnp.where(lane == k, codes[j * cap + k], note)
        boxes[j, 0, pl.ds(cap * tile, NOTE_ROWS)] = note.astype(jnp.float32).astype(boxes.dtype)
        copies_out[j].start()
    copies_in[1].wait()
    half_rows = masked.shape[1]
    for o in range(live.shape[0]):
        for c in range(live.shape[1]):
            lanes = pl.ds(c * tile, tile)
            kept = live[o, c].astype(jnp.float32)
            value = (plain[pl.ds(o * tile, tile), lanes].astype(jnp.float32) * kept).astype(
                masked.dtype
            )
            for first in range(o * tile, (o + 1) * tile, half_rows):
                rows_here = min(half_rows, tile)
                masked[first // half_rows, pl.ds(first % half_rows, rows_here), lanes] = value[
                    first - o * tile : first - o * tile + rows_here
                ]
    for copy in copies_out[n_v:]:
        copy.start()
    for copy in copies_out:
        copy.wait()


def read_notes(arrays, notes_wide, notes, sem):
    unit = 0
    for array in arrays:
        _, height, _ = array.shape
        for member in range(array.shape[0]):
            note = array[member, pl.ds(height - NOTE_ROWS, NOTE_ROWS)]
            notes_wide[pl.ds(unit, 1)] = note.astype(jnp.float32).astype(jnp.int32)[:1]
            unit += 1
    copy = pltpu.make_async_copy(notes_wide, notes, sem)
    copy.start()
    return copy


def clear_pairs(pairs):
    pairs[...] = jnp.zeros_like(pairs)


def add_unit(array, member, unit, blocks, cap, rows, notes, pairs, total):
    tile = array.shape[-1]

    def place(k):
        code = notes[unit, k]
        used = code >= 0
        row = jnp.where(used, lax.div(code, rows), 0)
        column = jnp.where(used, lax.rem(code, rows), rows)
        lanes = pl.ds(pl.multiple_of(row * tile, tile), tile)
        return jnp.concatenate([ref[index, :, lanes] for ref, index in blocks]), column

    for k in range(0, cap - 1, 2):
        pair = pairs.at[k // 2]
        pair[pl.ds(0, tile), pl.ds(0, tile)] = array[member, pl.ds(k * tile, tile)]
        pair[pl.ds(tile, tile), pl.ds(tile, tile)] = array[member, pl.ds((k + 1) * tile, tile)]
        (left, first), (right, second) = place(k), place(k + 1)
        both = jnp.dot(
            jnp.concatenate([left, right], axis=1),
            pair[...],
            preferred_element_type=jnp.float32,
        )
        total[first] += both[:, :tile]
        total[second] += both[:, tile:]
    if cap % 2:
        left, column = place(cap - 1)
        total[column] += jnp.dot(
            left,
            array[member, pl.ds((cap - 1) * tile, tile)],
            preferred_element_type=jnp.float32,
        )


def add_arrays(arrays, layout, amps, where, cap, rows, notes_wide, notes, pairs, total, sem):
    copy = read_notes(arrays, notes_wide, notes, sem)
    pairs[...] = jnp.zeros_like(pairs)
    total[...] = jnp.zeros_like(total)
    copy.wait()
    unit = 0
    for array, partners in zip(arrays, layout):
        for member, partner in enumerate(partners):
            blocks = [(amps[number], index) for number, index in where[partner]]
            add_unit(array, member, unit, blocks, cap, rows, notes, pairs, total)
            unit += 1


def split_refs(refs, *counts):
    parts = []
    for count in counts:
        parts.append(refs[:count])
        refs = refs[count:]
    return *parts, refs


def first_ladder_kernel(cap, layout, where, occupied, virtual, *refs):
    n_amps = 1 + max(number for blocks in where.values() for number, _ in blocks)
    amps, arrays, refs = split_refs(refs, n_amps, len(layout))
    total, occupied_out, inverse, *scratch = refs
    rows = total.shape[0] - 1
    add_arrays(arrays, layout, amps, where, cap, rows, *scratch[:3], total, scratch[3])
    tile = occupied_out.shape[-1]
    for o in range(occupied.shape[0]):
        here = pl.ds(o * tile, tile)
        column = jnp.broadcast_to(occupied[pl.ds(o, 1)], (tile, tile)).T
        occupied_out[here] = column
        for c in range(rows):
            lanes = pl.ds(c * tile, tile)
            inverse[here, lanes] = 1.0 / (column - virtual[:, lanes])


def middle_ladder_kernel(cap, layout, where, before, driver, amplitudes, occupied, virtual, *refs):
    n_amps = 1 + max(number for blocks in where.values() for number, _ in blocks)
    amps, arrays, refs = split_refs(refs, n_amps, len(layout))
    total, base, *scratch = refs
    rows = total.shape[0] - 1
    tile = occupied.shape[-1]
    add_arrays(arrays, layout, amps, where, cap, rows, *scratch[:3], total, scratch[3])
    total[...] += before[...]
    for c in range(rows):
        lanes = pl.ds(c * tile, tile)
        denominator = occupied[...] - virtual[:, lanes]
        plain = amplitudes[:, lanes].astype(jnp.float32)
        base[:, lanes] = driver[:, lanes].astype(jnp.float32) + denominator * plain


def last_ladder_kernel(cap, layout, where, before, base, *refs):
    n_amps = 1 + max(number for blocks in where.values() for number, _ in blocks)
    amps, arrays, refs = split_refs(refs, n_amps, len(layout))
    whole, twin, total, *scratch = refs
    rows, n_rows, tile = twin.shape
    add_arrays(arrays, layout, amps, where, cap, rows, *scratch[:3], total, scratch[3])
    twin[...] = (before[:rows, n_rows:] + total[:rows, n_rows:]).astype(twin.dtype)
    for c in range(rows):
        lanes = pl.ds(c * tile, tile)
        whole[:, lanes] = base[:, lanes] + before[c, :n_rows] + total[c, :n_rows]


def update_kernel(cap, partners, where, live, amplitudes, base, inverse, twin, *refs):
    n_amps = 1 + max(number for blocks in where.values() for number, _ in blocks)
    amps, arrays, outs, refs = split_refs(refs, n_amps, CORES, 2)
    new_buf, residual_buf, *scratch, total, sem, sems = refs
    rows, _, tile = twin.shape
    add_arrays(arrays, [partners] * CORES, amps, where, cap, rows, *scratch, total, sem)
    copies = []
    for c in range(rows):
        lanes = pl.ds(c * tile, tile)
        for o in range(live.shape[0]):
            here = pl.ds(o * tile, tile)
            at = (here, lanes)
            kept = live[o, c].astype(jnp.float32)
            masked = (amplitudes[at].astype(jnp.float32) * kept).astype(jnp.bfloat16)
            rest = (base[at] + (twin[c, here].astype(jnp.float32) + total[c, here])) * kept
            residual_buf[at] = rest
            new_buf[at] = (masked.astype(jnp.float32) - rest * inverse[at]).astype(new_buf.dtype)
        for i, source in enumerate((new_buf, residual_buf)):
            copies.append(
                pltpu.make_async_copy(source.at[:, lanes], outs[i].at[:, lanes], sems.at[i, c])
            )
            copies[-1].start()
    for copy in copies:
        copy.wait()


def on_device(
    amplitudes,
    tile_live,
    integrals,
    integral_columns,
    driver_terms,
    occupied_energy,
    virtual_energy,
):
    n_rows, width = amplitudes.shape
    rows, slots, tile, _ = integrals.shape
    n_v, n_o = lax.axis_size("vpair"), lax.axis_size("opair")
    n_z = n_o // CORES
    cap = -(-(rows * slots) // n_v)
    height = cap * tile + NOTE_ROWS
    dtype = integrals.dtype
    in_smem = pl.BlockSpec(memory_space=pltpu.SMEM)
    in_vmem = pl.BlockSpec(memory_space=pltpu.VMEM)
    anywhere = pl.BlockSpec(memory_space=pl.ANY)
    in_hbm = pl.BlockSpec(memory_space=pltpu.HBM)

    def after(values, others):
        return lax.optimization_barrier((values, others))[0]

    def params(*buffers):
        size = sum(math.prod(shape) * jnp.dtype(kind).itemsize for shape, kind in buffers)
        return pltpu.CompilerParams(vmem_limit_bytes=size + SPARE_VMEM)

    parcel = (1, height, tile)
    half = (n_rows // 2, width)
    *parcels, upper, lower = pl.pallas_call(
        functools.partial(pack_kernel, n_v, cap),
        out_shape=[jax.ShapeDtypeStruct(parcel, dtype)] * n_v
        + [jax.ShapeDtypeStruct(half, amplitudes.dtype)] * 2,
        in_specs=[in_smem, in_smem, in_hbm, in_hbm],
        out_specs=[in_hbm] * (n_v + 2),
        scratch_shapes=[pltpu.SMEM((n_v * cap,), jnp.int32)] * 2
        + [
            pltpu.VMEM(integrals.shape, dtype),
            pltpu.VMEM(amplitudes.shape, amplitudes.dtype),
            pltpu.VMEM((n_v, *parcel), dtype),
            pltpu.VMEM((2, *half), amplitudes.dtype),
            pltpu.SemaphoreType.DMA((2,)),
            pltpu.SemaphoreType.DMA((n_v + 2,)),
        ],
        compiler_params=pltpu.CompilerParams(vmem_limit_bytes=ALL_VMEM),
        name="pack",
    )(integral_columns.T, tile_live, integrals, amplitudes)

    def across_v(value, j):
        name = "amplitudes" if value.ndim == 2 else "parcels"
        with jax.named_scope(f"{name}_from_partner_{j}"):
            return lax.ppermute(value, "vpair", [(i, i ^ j) for i in range(n_v)])

    def across_core(value):
        return lax.ppermute(value, "opair", [(i, i ^ 1) for i in range(n_o)])

    def next_on_ring(value, name):
        ring = [*range(0, n_z, 2), *range(n_z - 1 - n_z % 2, 0, -2)]
        pairs = [
            (source * CORES + core, target * CORES + core)
            for source, target in zip(ring, ring[1:] + ring[:1])
            for core in range(CORES)
        ]
        with jax.named_scope(name):
            return lax.ppermute(value, "opair", pairs)

    def join(values):
        return jnp.concatenate(values) if len(values) > 1 else values[0]

    others = list(range(1, n_v))
    groups = {"near": [0], "early": others[: n_v // 2 - 1], "late": others[n_v // 2 - 1 :]}
    arrived = {0: parcels[0]} | {j: across_v(parcels[j], j) for j in others}
    hops = {name: [join([arrived[j] for j in groups[name]])] for name in groups}
    hops["near"].append(next_on_ring(hops["near"][0], "near_hop_1"))
    hops["early"][0] = after(hops["early"][0], hops["near"][1])
    hops["early"].append(next_on_ring(hops["early"][0], "early_hop_1"))
    hops["late"][0] = after(hops["late"][0], (hops["near"][1], hops["early"][0]))
    groups["first"] = groups["near"] + groups["early"]
    hops["late"].append(next_on_ring(hops["late"][0], "late_hop_1"))
    hops["first"] = [None, join([hops["near"][1], hops["early"][1]])]
    def gather_amplitudes(value, bits):
        pieces, own, twin = [value[None]], {0: (value[None], 0)}, {}
        ids = [0]
        for bit in bits:
            held = join(pieces)
            with jax.named_scope(f"amplitudes_bit_{bit}"):
                now = lax.ppermute(held, "vpair", [(i, i ^ bit) for i in range(n_v)])
            new_ids = [i ^ bit for i in ids]
            own |= {j: (now, i) for i, j in enumerate(new_ids)}
            with jax.named_scope(f"twin_of_bit_{bit}"):
                part, part_ids = (now, new_ids) if twin else (join([held, now]), ids + new_ids)
                swapped = across_core(after(part, hops["late"][1]))
            twin |= {j: (swapped, i) for i, j in enumerate(part_ids)}
            pieces.append(now)
            ids = ids + new_ids
        return own, twin

    bits = [1 << i for i in range((n_v - 1).bit_length())]
    upper, lower = after((upper, lower), (hops["late"][0], hops["early"][1]))
    upper_own, upper_twin = gather_amplitudes(upper, bits)
    lower_own, lower_twin = gather_amplitudes(lower, bits[::-1])

    def blocks_of(partners, *sources):
        amps, where = [], {}
        for j in partners:
            where[j] = []
            for source in sources:
                array, index = source[j]
                if not any(array is other for other in amps):
                    amps.append(array)
                number = [array is other for other in amps].index(True)
                where[j].append((number, index))
        return amps, where

    sums = (rows + 1, CORES * n_rows, tile)
    pairs = (max(cap // 2, 1), 2 * tile, 2 * tile)

    def ladder_call(kernel, found, before, out_shape, extra_scratch, flops, name):
        arrays, layout = [hops[name][hop] for name, hop in found], [groups[name] for name, _ in found]
        partners = sorted({j for part in layout for j in part})
        amps, where = blocks_of(partners, upper_own, lower_own, upper_twin, lower_twin)
        n_units = sum(len(part) for part in layout)
        return pl.pallas_call(
            functools.partial(kernel, cap, layout, where),
            out_shape=out_shape,
            in_specs=[in_vmem] * (len(before) + len(amps) + len(arrays)),
            out_specs=[in_vmem] * len(out_shape),
            scratch_shapes=extra_scratch
            + [
                pltpu.VMEM((n_units, tile), jnp.int32),
                pltpu.SMEM((n_units, tile), jnp.int32),
                pltpu.VMEM(pairs, dtype),
                pltpu.SemaphoreType.DMA,
            ],
            compiler_params=params(
                ((n_units, height, tile), dtype),
                *[(sums, jnp.float32)] * 4,
                ((n_v, CORES * n_rows, width), dtype),
            ),
            cost_estimate=pl.CostEstimate(
                flops=flops,
                bytes_accessed=1024 * 1024,
                transcendentals=0,
            ),
            name=name,
        )(*before, *amps, *arrays)

    virtual = virtual_energy.reshape(1, width)
    whole = jax.ShapeDtypeStruct((n_rows, width), jnp.float32)
    all_sums = jax.ShapeDtypeStruct(sums, jnp.float32)
    total, occupied, inverse = ladder_call(
        first_ladder_kernel,
        [("near", 0), ("early", 0), ("late", 0), ("first", 1), ("late", 1)],
        [occupied_energy.reshape(-1, tile), virtual],
        [all_sums, jax.ShapeDtypeStruct((n_rows, tile), jnp.float32), whole],
        [],
        FIRST_FLOPS,
        "ladder_first",
    )
    for hop in range(2, n_z):
        for name in ("first", "late"):
            hops[name].append(next_on_ring(hops[name][-1], f"{name}_hop_{hop}"))
    total, base = ladder_call(
        middle_ladder_kernel,
        [(name, hop) for hop in range(2, n_z - 1) for name in ("first", "late")],
        [total, driver_terms, amplitudes, occupied, virtual],
        [all_sums, whole],
        [],
        MIDDLE_FLOPS,
        "ladder_middle",
    )
    base, twin = ladder_call(
        last_ladder_kernel,
        [("first", n_z - 1)],
        [total, base],
        [whole, jax.ShapeDtypeStruct((rows, n_rows, tile), jnp.bfloat16)],
        [pltpu.VMEM(sums, jnp.float32)],
        LAST_FLOPS,
        "ladder_last",
    )
    last, behind = after(hops["late"][-1], twin), groups["late"]
    twin = across_core(twin)

    n_last = CORES * len(behind)
    amps, where = blocks_of(behind, upper_own, lower_own)
    sums = (rows + 1, n_rows, tile)
    return pl.pallas_call(
        functools.partial(update_kernel, cap, behind, where),
        out_shape=[
            jax.ShapeDtypeStruct((n_rows, width), jnp.bfloat16),
            jax.ShapeDtypeStruct((n_rows, width), jnp.float32),
        ],
        in_specs=[in_smem] + [in_vmem] * (4 + len(amps) + CORES),
        out_specs=[in_hbm] * 2,
        scratch_shapes=[
            pltpu.VMEM((n_rows, width), jnp.bfloat16),
            pltpu.VMEM((n_rows, width), jnp.float32),
            pltpu.VMEM((n_last, tile), jnp.int32),
            pltpu.SMEM((n_last, tile), jnp.int32),
            pltpu.VMEM(pairs, dtype),
            pltpu.VMEM(sums, jnp.float32),
            pltpu.SemaphoreType.DMA,
            pltpu.SemaphoreType.DMA((2, rows)),
        ],
        compiler_params=params(
            ((n_v, n_rows, width), dtype), ((n_last, height, tile), dtype), *[(sums, jnp.float32)] * 5
        ),
        name="update",
    )(
        tile_live,
        amplitudes,
        base,
        inverse,
        twin,
        *amps,
        last,
        across_core(last),
    )


def solution(mesh):
    in_specs = (
        P("opair", "vpair"),
        P("opair", "vpair"),
        P("vpair", "opair", None, None),
        P("vpair", "opair"),
        P("opair", "vpair"),
        P("opair"),
        P("vpair"),
    )
    out_specs = (P("opair", "vpair"), P("opair", "vpair"))
    return jax.shard_map(
        on_device, mesh=mesh, in_specs=in_specs, out_specs=out_specs, check_vma=False
    )
```

```python
import functools
import math

import jax
import jax.numpy as jnp
from jax import lax
from jax.experimental import pallas as pl
from jax.experimental.pallas import tpu as pltpu
from jax.sharding import PartitionSpec as P

SPARE_VMEM = 4 * 1024 * 1024
ALL_VMEM = 60 * 1024 * 1024
CORES = 2
NOTE_ROWS = 16
FIRST_FLOPS = 10**9
MIDDLE_FLOPS = 10**8
LAST_FLOPS = 10**9


def pack_kernel(n_v, cap, columns, live, integrals, amplitudes, *refs):
    parcels, halves, refs = refs[:n_v], refs[n_v : n_v + 2], refs[n_v + 2 :]
    origin, codes, tiles, plain, boxes, masked, in_sems, out_sems = refs
    rows, slots, tile, _ = integrals.shape
    me = lax.axis_index("vpair")
    copies_in = [
        pltpu.make_async_copy(integrals, tiles, in_sems.at[0]),
        pltpu.make_async_copy(amplitudes, plain, in_sems.at[1]),
    ]
    copies_out = [pltpu.make_async_copy(boxes.at[j], parcels[j], out_sems.at[j]) for j in range(n_v)]
    copies_out += [
        pltpu.make_async_copy(masked.at[i], halves[i], out_sems.at[n_v + i]) for i in range(2)
    ]
    for copy in copies_in:
        copy.start()
    counts = [jnp.int32(0)] * n_v
    for i in range(n_v * cap):
        origin[i] = 0
        codes[i] = -1
    for row in range(rows):
        for slot in range(slots):
            column = columns[slot, row]
            partner = lax.div(column, rows) ^ me
            place = counts[0]
            for j in range(1, n_v):
                place = jnp.where(partner == j, counts[j], place)
            counts = [counts[j] + (partner == j).astype(jnp.int32) for j in range(n_v)]
            at = partner * cap + place
            origin[at] = row * slots + slot
            codes[at] = row * rows + lax.rem(column, rows)
    copies_in[0].wait()
    lane = lax.broadcasted_iota(jnp.int32, (NOTE_ROWS, tile), 1)
    for j in range(n_v):
        note = jnp.full((NOTE_ROWS, tile), -1, jnp.int32)
        for k in range(cap):
            entry = origin[j * cap + k]
            boxes[j, 0, pl.ds(k * tile, tile)] = tiles[
                lax.div(entry, slots), lax.rem(entry, slots)
            ]
            note = jnp.where(lane == k, codes[j * cap + k], note)
        boxes[j, 0, pl.ds(cap * tile, NOTE_ROWS)] = note.astype(jnp.float32).astype(boxes.dtype)
        copies_out[j].start()
    copies_in[1].wait()
    half_rows = masked.shape[1]
    for o in range(live.shape[0]):
        for c in range(live.shape[1]):
            lanes = pl.ds(c * tile, tile)
            kept = live[o, c].astype(jnp.float32)
            value = (plain[pl.ds(o * tile, tile), lanes].astype(jnp.float32) * kept).astype(
                masked.dtype
            )
            for first in range(o * tile, (o + 1) * tile, half_rows):
                rows_here = min(half_rows, tile)
                masked[first // half_rows, pl.ds(first % half_rows, rows_here), lanes] = value[
                    first - o * tile : first - o * tile + rows_here
                ]
    for copy in copies_out[n_v:]:
        copy.start()
    for copy in copies_out:
        copy.wait()


def read_notes(arrays, notes_wide, notes, sem):
    unit = 0
    for array in arrays:
        _, height, _ = array.shape
        for member in range(array.shape[0]):
            note = array[member, pl.ds(height - NOTE_ROWS, NOTE_ROWS)]
            notes_wide[pl.ds(unit, 1)] = note.astype(jnp.float32).astype(jnp.int32)[:1]
            unit += 1
    copy = pltpu.make_async_copy(notes_wide, notes, sem)
    copy.start()
    return copy


def clear_pairs(pairs):
    pairs[...] = jnp.zeros_like(pairs)


def add_unit(array, member, unit, blocks, cap, rows, notes, pairs, total):
    tile = array.shape[-1]

    def place(k):
        code = notes[unit, k]
        used = code >= 0
        row = jnp.where(used, lax.div(code, rows), 0)
        column = jnp.where(used, lax.rem(code, rows), rows)
        lanes = pl.ds(pl.multiple_of(row * tile, tile), tile)
        return jnp.concatenate([ref[index, :, lanes] for ref, index in blocks]), column

    for k in range(0, cap - 1, 2):
        pair = pairs.at[k // 2]
        pair[pl.ds(0, tile), pl.ds(0, tile)] = array[member, pl.ds(k * tile, tile)]
        pair[pl.ds(tile, tile), pl.ds(tile, tile)] = array[member, pl.ds((k + 1) * tile, tile)]
        (left, first), (right, second) = place(k), place(k + 1)
        both = jnp.dot(
            jnp.concatenate([left, right], axis=1),
            pair[...],
            preferred_element_type=jnp.float32,
        )
        total[first] += both[:, :tile]
        total[second] += both[:, tile:]
    if cap % 2:
        left, column = place(cap - 1)
        total[column] += jnp.dot(
            left,
            array[member, pl.ds((cap - 1) * tile, tile)],
            preferred_element_type=jnp.float32,
        )


def add_arrays(arrays, layout, amps, where, cap, rows, notes_wide, notes, pairs, total, sem):
    copy = read_notes(arrays, notes_wide, notes, sem)
    pairs[...] = jnp.zeros_like(pairs)
    total[...] = jnp.zeros_like(total)
    copy.wait()
    unit = 0
    for array, partners in zip(arrays, layout):
        for member, partner in enumerate(partners):
            blocks = [(amps[number], index) for number, index in where[partner]]
            add_unit(array, member, unit, blocks, cap, rows, notes, pairs, total)
            unit += 1


def split_refs(refs, *counts):
    parts = []
    for count in counts:
        parts.append(refs[:count])
        refs = refs[count:]
    return *parts, refs


def first_ladder_kernel(cap, layout, where, occupied, virtual, *refs):
    n_amps = 1 + max(number for blocks in where.values() for number, _ in blocks)
    amps, arrays, refs = split_refs(refs, n_amps, len(layout))
    total, occupied_out, inverse, *scratch = refs
    rows = total.shape[0] - 1
    add_arrays(arrays, layout, amps, where, cap, rows, *scratch[:3], total, scratch[3])
    tile = occupied_out.shape[-1]
    for o in range(occupied.shape[0]):
        here = pl.ds(o * tile, tile)
        column = jnp.broadcast_to(occupied[pl.ds(o, 1)], (tile, tile)).T
        occupied_out[here] = column
        for c in range(rows):
            lanes = pl.ds(c * tile, tile)
            inverse[here, lanes] = 1.0 / (column - virtual[:, lanes])


def middle_ladder_kernel(cap, layout, where, before, driver, amplitudes, occupied, virtual, *refs):
    n_amps = 1 + max(number for blocks in where.values() for number, _ in blocks)
    amps, arrays, refs = split_refs(refs, n_amps, len(layout))
    total, base, *scratch = refs
    rows = total.shape[0] - 1
    tile = occupied.shape[-1]
    add_arrays(arrays, layout, amps, where, cap, rows, *scratch[:3], total, scratch[3])
    total[...] += before[...]
    for c in range(rows):
        lanes = pl.ds(c * tile, tile)
        denominator = occupied[...] - virtual[:, lanes]
        plain = amplitudes[:, lanes].astype(jnp.float32)
        base[:, lanes] = driver[:, lanes].astype(jnp.float32) + denominator * plain


def last_ladder_kernel(cap, layout, where, before, base, *refs):
    n_amps = 1 + max(number for blocks in where.values() for number, _ in blocks)
    amps, arrays, refs = split_refs(refs, n_amps, len(layout))
    whole, twin, total, *scratch = refs
    rows, n_rows, tile = twin.shape
    add_arrays(arrays, layout, amps, where, cap, rows, *scratch[:3], total, scratch[3])
    twin[...] = (before[:rows, n_rows:] + total[:rows, n_rows:]).astype(twin.dtype)
    for c in range(rows):
        lanes = pl.ds(c * tile, tile)
        whole[:, lanes] = base[:, lanes] + before[c, :n_rows] + total[c, :n_rows]


def update_kernel(cap, partners, where, live, amplitudes, base, inverse, twin, *refs):
    n_amps = 1 + max(number for blocks in where.values() for number, _ in blocks)
    amps, arrays, outs, refs = split_refs(refs, n_amps, CORES, 2)
    new_buf, residual_buf, *scratch, total, sem, sems = refs
    rows, _, tile = twin.shape
    add_arrays(arrays, [partners] * CORES, amps, where, cap, rows, *scratch, total, sem)
    copies = []
    for c in range(rows):
        lanes = pl.ds(c * tile, tile)
        for o in range(live.shape[0]):
            here = pl.ds(o * tile, tile)
            at = (here, lanes)
            kept = live[o, c].astype(jnp.float32)
            masked = (amplitudes[at].astype(jnp.float32) * kept).astype(jnp.bfloat16)
            rest = (base[at] + (twin[c, here].astype(jnp.float32) + total[c, here])) * kept
            residual_buf[at] = rest
            new_buf[at] = (masked.astype(jnp.float32) - rest * inverse[at]).astype(new_buf.dtype)
        for i, source in enumerate((new_buf, residual_buf)):
            copies.append(
                pltpu.make_async_copy(source.at[:, lanes], outs[i].at[:, lanes], sems.at[i, c])
            )
            copies[-1].start()
    for copy in copies:
        copy.wait()


def on_device(
    amplitudes,
    tile_live,
    integrals,
    integral_columns,
    driver_terms,
    occupied_energy,
    virtual_energy,
):
    n_rows, width = amplitudes.shape
    rows, slots, tile, _ = integrals.shape
    n_v, n_o = lax.axis_size("vpair"), lax.axis_size("opair")
    n_z = n_o // CORES
    cap = -(-(rows * slots) // n_v)
    height = cap * tile + NOTE_ROWS
    dtype = integrals.dtype
    in_smem = pl.BlockSpec(memory_space=pltpu.SMEM)
    in_vmem = pl.BlockSpec(memory_space=pltpu.VMEM)
    anywhere = pl.BlockSpec(memory_space=pl.ANY)
    in_hbm = pl.BlockSpec(memory_space=pltpu.HBM)

    def after(values, others):
        return lax.optimization_barrier((values, others))[0]

    def params(*buffers):
        size = sum(math.prod(shape) * jnp.dtype(kind).itemsize for shape, kind in buffers)
        return pltpu.CompilerParams(vmem_limit_bytes=size + SPARE_VMEM)

    parcel = (1, height, tile)
    half = (n_rows // 2, width)
    *parcels, upper, lower = pl.pallas_call(
        functools.partial(pack_kernel, n_v, cap),
        out_shape=[jax.ShapeDtypeStruct(parcel, dtype)] * n_v
        + [jax.ShapeDtypeStruct(half, amplitudes.dtype)] * 2,
        in_specs=[in_smem, in_smem, in_hbm, in_hbm],
        out_specs=[in_hbm] * (n_v + 2),
        scratch_shapes=[pltpu.SMEM((n_v * cap,), jnp.int32)] * 2
        + [
            pltpu.VMEM(integrals.shape, dtype),
            pltpu.VMEM(amplitudes.shape, amplitudes.dtype),
            pltpu.VMEM((n_v, *parcel), dtype),
            pltpu.VMEM((2, *half), amplitudes.dtype),
            pltpu.SemaphoreType.DMA((2,)),
            pltpu.SemaphoreType.DMA((n_v + 2,)),
        ],
        compiler_params=pltpu.CompilerParams(vmem_limit_bytes=ALL_VMEM),
        name="pack",
    )(integral_columns.T, tile_live, integrals, amplitudes)

    def across_v(value, j):
        name = "amplitudes" if value.ndim == 2 else "parcels"
        with jax.named_scope(f"{name}_from_partner_{j}"):
            return lax.ppermute(value, "vpair", [(i, i ^ j) for i in range(n_v)])

    def across_core(value):
        return lax.ppermute(value, "opair", [(i, i ^ 1) for i in range(n_o)])

    def next_on_ring(value, name):
        ring = [*range(0, n_z, 2), *range(n_z - 1 - n_z % 2, 0, -2)]
        pairs = [
            (source * CORES + core, target * CORES + core)
            for source, target in zip(ring, ring[1:] + ring[:1])
            for core in range(CORES)
        ]
        with jax.named_scope(name):
            return lax.ppermute(value, "opair", pairs)

    def join(values):
        return jnp.concatenate(values) if len(values) > 1 else values[0]

    others = list(range(1, n_v))
    groups = {"near": [0], "early": others[: n_v // 2 - 1], "late": others[n_v // 2 - 1 :]}
    arrived = {0: parcels[0]} | {j: across_v(parcels[j], j) for j in others}
    hops = {name: [join([arrived[j] for j in groups[name]])] for name in groups}
    hops["near"].append(next_on_ring(hops["near"][0], "near_hop_1"))
    hops["early"][0] = after(hops["early"][0], hops["near"][1])
    hops["early"].append(next_on_ring(hops["early"][0], "early_hop_1"))
    hops["late"][0] = after(hops["late"][0], (hops["near"][1], hops["early"][0]))
    groups["first"] = groups["near"] + groups["early"]
    hops["late"].append(next_on_ring(hops["late"][0], "late_hop_1"))
    hops["first"] = [None, join([hops["near"][1], hops["early"][1]])]
    def gather_amplitudes(value, bits):
        pieces, own, twin = [value[None]], {0: (value[None], 0)}, {}
        ids = [0]
        for bit in bits:
            held = join(pieces)
            with jax.named_scope(f"amplitudes_bit_{bit}"):
                now = lax.ppermute(held, "vpair", [(i, i ^ bit) for i in range(n_v)])
            new_ids = [i ^ bit for i in ids]
            own |= {j: (now, i) for i, j in enumerate(new_ids)}
            with jax.named_scope(f"twin_of_bit_{bit}"):
                part, part_ids = (now, new_ids) if twin else (join([held, now]), ids + new_ids)
                swapped = across_core(after(part, hops["late"][1]))
            twin |= {j: (swapped, i) for i, j in enumerate(part_ids)}
            pieces.append(now)
            ids = ids + new_ids
        return own, twin

    bits = [1 << i for i in range((n_v - 1).bit_length())]
    upper, lower = after((upper, lower), hops["near"][1])
    upper_own, upper_twin = gather_amplitudes(upper, bits)
    lower_own, lower_twin = gather_amplitudes(lower, bits[::-1])

    def blocks_of(partners, *sources):
        amps, where = [], {}
        for j in partners:
            where[j] = []
            for source in sources:
                array, index = source[j]
                if not any(array is other for other in amps):
                    amps.append(array)
                number = [array is other for other in amps].index(True)
                where[j].append((number, index))
        return amps, where

    sums = (rows + 1, CORES * n_rows, tile)
    pairs = (max(cap // 2, 1), 2 * tile, 2 * tile)

    def ladder_call(kernel, found, before, out_shape, extra_scratch, flops, name):
        arrays, layout = [hops[name][hop] for name, hop in found], [groups[name] for name, _ in found]
        partners = sorted({j for part in layout for j in part})
        amps, where = blocks_of(partners, upper_own, lower_own, upper_twin, lower_twin)
        n_units = sum(len(part) for part in layout)
        return pl.pallas_call(
            functools.partial(kernel, cap, layout, where),
            out_shape=out_shape,
            in_specs=[in_vmem] * (len(before) + len(amps) + len(arrays)),
            out_specs=[in_vmem] * len(out_shape),
            scratch_shapes=extra_scratch
            + [
                pltpu.VMEM((n_units, tile), jnp.int32),
                pltpu.SMEM((n_units, tile), jnp.int32),
                pltpu.VMEM(pairs, dtype),
                pltpu.SemaphoreType.DMA,
            ],
            compiler_params=params(
                ((n_units, height, tile), dtype),
                *[(sums, jnp.float32)] * 4,
                ((n_v, CORES * n_rows, width), dtype),
            ),
            cost_estimate=pl.CostEstimate(
                flops=flops,
                bytes_accessed=1024 * 1024,
                transcendentals=0,
            ),
            name=name,
        )(*before, *amps, *arrays)

    virtual = virtual_energy.reshape(1, width)
    whole = jax.ShapeDtypeStruct((n_rows, width), jnp.float32)
    all_sums = jax.ShapeDtypeStruct(sums, jnp.float32)
    total, occupied, inverse = ladder_call(
        first_ladder_kernel,
        [("near", 0), ("early", 0), ("late", 0), ("first", 1), ("late", 1)],
        [occupied_energy.reshape(-1, tile), virtual],
        [all_sums, jax.ShapeDtypeStruct((n_rows, tile), jnp.float32), whole],
        [],
        FIRST_FLOPS,
        "ladder_first",
    )
    for hop in range(2, n_z):
        for name in ("first", "late"):
            hops[name].append(next_on_ring(hops[name][-1], f"{name}_hop_{hop}"))
    total, base = ladder_call(
        middle_ladder_kernel,
        [(name, hop) for hop in range(2, n_z - 1) for name in ("first", "late")],
        [total, driver_terms, amplitudes, occupied, virtual],
        [all_sums, whole],
        [],
        MIDDLE_FLOPS,
        "ladder_middle",
    )
    base, twin = ladder_call(
        last_ladder_kernel,
        [("first", n_z - 1)],
        [total, base],
        [whole, jax.ShapeDtypeStruct((rows, n_rows, tile), jnp.bfloat16)],
        [pltpu.VMEM(sums, jnp.float32)],
        LAST_FLOPS,
        "ladder_last",
    )
    last, behind = after(hops["late"][-1], twin), groups["late"]
    twin = across_core(twin)

    n_last = CORES * len(behind)
    amps, where = blocks_of(behind, upper_own, lower_own)
    sums = (rows + 1, n_rows, tile)
    return pl.pallas_call(
        functools.partial(update_kernel, cap, behind, where),
        out_shape=[
            jax.ShapeDtypeStruct((n_rows, width), jnp.bfloat16),
            jax.ShapeDtypeStruct((n_rows, width), jnp.float32),
        ],
        in_specs=[in_smem] + [in_vmem] * (4 + len(amps) + CORES),
        out_specs=[in_hbm] * 2,
        scratch_shapes=[
            pltpu.VMEM((n_rows, width), jnp.bfloat16),
            pltpu.VMEM((n_rows, width), jnp.float32),
            pltpu.VMEM((n_last, tile), jnp.int32),
            pltpu.SMEM((n_last, tile), jnp.int32),
            pltpu.VMEM(pairs, dtype),
            pltpu.VMEM(sums, jnp.float32),
            pltpu.SemaphoreType.DMA,
            pltpu.SemaphoreType.DMA((2, rows)),
        ],
        compiler_params=params(
            ((n_v, n_rows, width), dtype), ((n_last, height, tile), dtype), *[(sums, jnp.float32)] * 5
        ),
        name="update",
    )(
        tile_live,
        amplitudes,
        base,
        inverse,
        twin,
        *amps,
        last,
        across_core(last),
    )


def solution(mesh):
    in_specs = (
        P("opair", "vpair"),
        P("opair", "vpair"),
        P("vpair", "opair", None, None),
        P("vpair", "opair"),
        P("opair", "vpair"),
        P("opair"),
        P("vpair"),
    )
    out_specs = (P("opair", "vpair"), P("opair", "vpair"))
    return jax.shard_map(
        on_device, mesh=mesh, in_specs=in_specs, out_specs=out_specs, check_vma=False
    )
```

```python
import functools
import math

import jax
import jax.numpy as jnp
from jax import lax
from jax.experimental import pallas as pl
from jax.experimental.pallas import tpu as pltpu
from jax.sharding import PartitionSpec as P

SPARE_VMEM = 4 * 1024 * 1024
ALL_VMEM = 60 * 1024 * 1024
CORES = 2
NOTE_ROWS = 16
FIRST_FLOPS = 10**6
MIDDLE_FLOPS = 10**8
LAST_FLOPS = 10**9


def pack_kernel(n_v, cap, columns, live, integrals, amplitudes, *refs):
    parcels, halves, refs = refs[:n_v], refs[n_v : n_v + 2], refs[n_v + 2 :]
    origin, codes, tiles, plain, boxes, masked, in_sems, out_sems = refs
    rows, slots, tile, _ = integrals.shape
    me = lax.axis_index("vpair")
    copies_in = [
        pltpu.make_async_copy(integrals, tiles, in_sems.at[0]),
        pltpu.make_async_copy(amplitudes, plain, in_sems.at[1]),
    ]
    copies_out = [pltpu.make_async_copy(boxes.at[j], parcels[j], out_sems.at[j]) for j in range(n_v)]
    copies_out += [
        pltpu.make_async_copy(masked.at[i], halves[i], out_sems.at[n_v + i]) for i in range(2)
    ]
    for copy in copies_in:
        copy.start()
    counts = [jnp.int32(0)] * n_v
    for i in range(n_v * cap):
        origin[i] = 0
        codes[i] = -1
    for row in range(rows):
        for slot in range(slots):
            column = columns[slot, row]
            partner = lax.div(column, rows) ^ me
            place = counts[0]
            for j in range(1, n_v):
                place = jnp.where(partner == j, counts[j], place)
            counts = [counts[j] + (partner == j).astype(jnp.int32) for j in range(n_v)]
            at = partner * cap + place
            origin[at] = row * slots + slot
            codes[at] = row * rows + lax.rem(column, rows)
    copies_in[0].wait()
    lane = lax.broadcasted_iota(jnp.int32, (NOTE_ROWS, tile), 1)
    for j in range(n_v):
        note = jnp.full((NOTE_ROWS, tile), -1, jnp.int32)
        for k in range(cap):
            entry = origin[j * cap + k]
            boxes[j, 0, pl.ds(k * tile, tile)] = tiles[
                lax.div(entry, slots), lax.rem(entry, slots)
            ]
            note = jnp.where(lane == k, codes[j * cap + k], note)
        boxes[j, 0, pl.ds(cap * tile, NOTE_ROWS)] = note.astype(jnp.float32).astype(boxes.dtype)
        copies_out[j].start()
    copies_in[1].wait()
    half_rows = masked.shape[1]
    for o in range(live.shape[0]):
        for c in range(live.shape[1]):
            lanes = pl.ds(c * tile, tile)
            kept = live[o, c].astype(jnp.float32)
            value = (plain[pl.ds(o * tile, tile), lanes].astype(jnp.float32) * kept).astype(
                masked.dtype
            )
            for first in range(o * tile, (o + 1) * tile, half_rows):
                rows_here = min(half_rows, tile)
                masked[first // half_rows, pl.ds(first % half_rows, rows_here), lanes] = value[
                    first - o * tile : first - o * tile + rows_here
                ]
    for copy in copies_out[n_v:]:
        copy.start()
    for copy in copies_out:
        copy.wait()


def read_notes(arrays, notes_wide, notes, sem):
    unit = 0
    for array in arrays:
        _, height, _ = array.shape
        for member in range(array.shape[0]):
            note = array[member, pl.ds(height - NOTE_ROWS, NOTE_ROWS)]
            notes_wide[pl.ds(unit, 1)] = note.astype(jnp.float32).astype(jnp.int32)[:1]
            unit += 1
    copy = pltpu.make_async_copy(notes_wide, notes, sem)
    copy.start()
    return copy


def clear_pairs(pairs):
    pairs[...] = jnp.zeros_like(pairs)


def add_unit(array, member, unit, blocks, cap, rows, notes, pairs, total):
    tile = array.shape[-1]

    def place(k):
        code = notes[unit, k]
        used = code >= 0
        row = jnp.where(used, lax.div(code, rows), 0)
        column = jnp.where(used, lax.rem(code, rows), rows)
        lanes = pl.ds(pl.multiple_of(row * tile, tile), tile)
        return jnp.concatenate([ref[index, :, lanes] for ref, index in blocks]), column

    for k in range(0, cap - 1, 2):
        pair = pairs.at[k // 2]
        pair[pl.ds(0, tile), pl.ds(0, tile)] = array[member, pl.ds(k * tile, tile)]
        pair[pl.ds(tile, tile), pl.ds(tile, tile)] = array[member, pl.ds((k + 1) * tile, tile)]
        (left, first), (right, second) = place(k), place(k + 1)
        both = jnp.dot(
            jnp.concatenate([left, right], axis=1),
            pair[...],
            preferred_element_type=jnp.float32,
        )
        total[first] += both[:, :tile]
        total[second] += both[:, tile:]
    if cap % 2:
        left, column = place(cap - 1)
        total[column] += jnp.dot(
            left,
            array[member, pl.ds((cap - 1) * tile, tile)],
            preferred_element_type=jnp.float32,
        )


def add_arrays(arrays, layout, amps, where, cap, rows, notes_wide, notes, pairs, total, sem):
    copy = read_notes(arrays, notes_wide, notes, sem)
    pairs[...] = jnp.zeros_like(pairs)
    total[...] = jnp.zeros_like(total)
    copy.wait()
    unit = 0
    for array, partners in zip(arrays, layout):
        for member, partner in enumerate(partners):
            blocks = [(amps[number], index) for number, index in where[partner]]
            add_unit(array, member, unit, blocks, cap, rows, notes, pairs, total)
            unit += 1


def split_refs(refs, *counts):
    parts = []
    for count in counts:
        parts.append(refs[:count])
        refs = refs[count:]
    return *parts, refs


def first_ladder_kernel(cap, layout, where, occupied, virtual, *refs):
    n_amps = 1 + max(number for blocks in where.values() for number, _ in blocks)
    amps, arrays, refs = split_refs(refs, n_amps, len(layout))
    total, occupied_out, inverse, *scratch = refs
    rows = total.shape[0] - 1
    add_arrays(arrays, layout, amps, where, cap, rows, *scratch[:3], total, scratch[3])
    tile = occupied_out.shape[-1]
    for o in range(occupied.shape[0]):
        here = pl.ds(o * tile, tile)
        column = jnp.broadcast_to(occupied[pl.ds(o, 1)], (tile, tile)).T
        occupied_out[here] = column
        for c in range(rows):
            lanes = pl.ds(c * tile, tile)
            inverse[here, lanes] = 1.0 / (column - virtual[:, lanes])


def middle_ladder_kernel(cap, layout, where, before, driver, amplitudes, occupied, virtual, *refs):
    n_amps = 1 + max(number for blocks in where.values() for number, _ in blocks)
    amps, arrays, refs = split_refs(refs, n_amps, len(layout))
    total, base, *scratch = refs
    rows = total.shape[0] - 1
    tile = occupied.shape[-1]
    add_arrays(arrays, layout, amps, where, cap, rows, *scratch[:3], total, scratch[3])
    total[...] += before[...]
    for c in range(rows):
        lanes = pl.ds(c * tile, tile)
        denominator = occupied[...] - virtual[:, lanes]
        plain = amplitudes[:, lanes].astype(jnp.float32)
        base[:, lanes] = driver[:, lanes].astype(jnp.float32) + denominator * plain


def last_ladder_kernel(cap, layout, where, before, base, *refs):
    n_amps = 1 + max(number for blocks in where.values() for number, _ in blocks)
    amps, arrays, refs = split_refs(refs, n_amps, len(layout))
    whole, twin, total, *scratch = refs
    rows, n_rows, tile = twin.shape
    add_arrays(arrays, layout, amps, where, cap, rows, *scratch[:3], total, scratch[3])
    twin[...] = (before[:rows, n_rows:] + total[:rows, n_rows:]).astype(twin.dtype)
    for c in range(rows):
        lanes = pl.ds(c * tile, tile)
        whole[:, lanes] = base[:, lanes] + before[c, :n_rows] + total[c, :n_rows]


def update_kernel(cap, partners, where, live, amplitudes, base, inverse, twin, *refs):
    n_amps = 1 + max(number for blocks in where.values() for number, _ in blocks)
    amps, arrays, outs, refs = split_refs(refs, n_amps, CORES, 2)
    new_buf, residual_buf, *scratch, total, sem, sems = refs
    rows, _, tile = twin.shape
    add_arrays(arrays, [partners] * CORES, amps, where, cap, rows, *scratch, total, sem)
    copies = []
    for c in range(rows):
        lanes = pl.ds(c * tile, tile)
        for o in range(live.shape[0]):
            here = pl.ds(o * tile, tile)
            at = (here, lanes)
            kept = live[o, c].astype(jnp.float32)
            masked = (amplitudes[at].astype(jnp.float32) * kept).astype(jnp.bfloat16)
            rest = (base[at] + (twin[c, here].astype(jnp.float32) + total[c, here])) * kept
            residual_buf[at] = rest
            new_buf[at] = (masked.astype(jnp.float32) - rest * inverse[at]).astype(new_buf.dtype)
        for i, source in enumerate((new_buf, residual_buf)):
            copies.append(
                pltpu.make_async_copy(source.at[:, lanes], outs[i].at[:, lanes], sems.at[i, c])
            )
            copies[-1].start()
    for copy in copies:
        copy.wait()


def on_device(
    amplitudes,
    tile_live,
    integrals,
    integral_columns,
    driver_terms,
    occupied_energy,
    virtual_energy,
):
    n_rows, width = amplitudes.shape
    rows, slots, tile, _ = integrals.shape
    n_v, n_o = lax.axis_size("vpair"), lax.axis_size("opair")
    n_z = n_o // CORES
    cap = -(-(rows * slots) // n_v)
    height = cap * tile + NOTE_ROWS
    dtype = integrals.dtype
    in_smem = pl.BlockSpec(memory_space=pltpu.SMEM)
    in_vmem = pl.BlockSpec(memory_space=pltpu.VMEM)
    anywhere = pl.BlockSpec(memory_space=pl.ANY)
    in_hbm = pl.BlockSpec(memory_space=pltpu.HBM)

    def after(values, others):
        return lax.optimization_barrier((values, others))[0]

    def params(*buffers):
        size = sum(math.prod(shape) * jnp.dtype(kind).itemsize for shape, kind in buffers)
        return pltpu.CompilerParams(vmem_limit_bytes=size + SPARE_VMEM)

    parcel = (1, height, tile)
    half = (n_rows // 2, width)
    *parcels, upper, lower = pl.pallas_call(
        functools.partial(pack_kernel, n_v, cap),
        out_shape=[jax.ShapeDtypeStruct(parcel, dtype)] * n_v
        + [jax.ShapeDtypeStruct(half, amplitudes.dtype)] * 2,
        in_specs=[in_smem, in_smem, in_hbm, in_hbm],
        out_specs=[in_hbm] * (n_v + 2),
        scratch_shapes=[pltpu.SMEM((n_v * cap,), jnp.int32)] * 2
        + [
            pltpu.VMEM(integrals.shape, dtype),
            pltpu.VMEM(amplitudes.shape, amplitudes.dtype),
            pltpu.VMEM((n_v, *parcel), dtype),
            pltpu.VMEM((2, *half), amplitudes.dtype),
            pltpu.SemaphoreType.DMA((2,)),
            pltpu.SemaphoreType.DMA((n_v + 2,)),
        ],
        compiler_params=pltpu.CompilerParams(vmem_limit_bytes=ALL_VMEM),
        name="pack",
    )(integral_columns.T, tile_live, integrals, amplitudes)

    def across_v(value, j):
        name = "amplitudes" if value.ndim == 2 else "parcels"
        with jax.named_scope(f"{name}_from_partner_{j}"):
            return lax.ppermute(value, "vpair", [(i, i ^ j) for i in range(n_v)])

    def across_core(value):
        return lax.ppermute(value, "opair", [(i, i ^ 1) for i in range(n_o)])

    def next_on_ring(value, name):
        ring = [*range(0, n_z, 2), *range(n_z - 1 - n_z % 2, 0, -2)]
        pairs = [
            (source * CORES + core, target * CORES + core)
            for source, target in zip(ring, ring[1:] + ring[:1])
            for core in range(CORES)
        ]
        with jax.named_scope(name):
            return lax.ppermute(value, "opair", pairs)

    def join(values):
        return jnp.concatenate(values) if len(values) > 1 else values[0]

    others = list(range(1, n_v))
    groups = {"near": [0], "early": others[: n_v // 2 - 1], "late": others[n_v // 2 - 1 :]}
    arrived = {0: parcels[0]} | {j: across_v(parcels[j], j) for j in others}
    hops = {name: [join([arrived[j] for j in groups[name]])] for name in groups}
    hops["near"].append(next_on_ring(hops["near"][0], "near_hop_1"))
    hops["early"][0] = after(hops["early"][0], hops["near"][1])
    hops["early"].append(next_on_ring(hops["early"][0], "early_hop_1"))
    hops["late"][0] = after(hops["late"][0], (hops["near"][1], hops["early"][0]))
    groups["first"] = groups["near"] + groups["early"]
    hops["late"].append(next_on_ring(hops["late"][0], "late_hop_1"))
    hops["first"] = [None, join([hops["near"][1], hops["early"][1]])]
    def gather_amplitudes(value, bits):
        pieces, own, twin = [value[None]], {0: (value[None], 0)}, {}
        ids = [0]
        for bit in bits:
            held = after(join(pieces), hops["early"][1]) if twin else join(pieces)
            with jax.named_scope(f"amplitudes_bit_{bit}"):
                now = lax.ppermute(held, "vpair", [(i, i ^ bit) for i in range(n_v)])
            new_ids = [i ^ bit for i in ids]
            own |= {j: (now, i) for i, j in enumerate(new_ids)}
            with jax.named_scope(f"twin_of_bit_{bit}"):
                part, part_ids = (now, new_ids) if twin else (join([held, now]), ids + new_ids)
                swapped = across_core(part)
            twin |= {j: (swapped, i) for i, j in enumerate(part_ids)}
            pieces.append(now)
            ids = ids + new_ids
        return own, twin

    bits = [1 << i for i in range((n_v - 1).bit_length())]
    upper, lower = after((upper, lower), hops["near"][1])
    upper_own, upper_twin = gather_amplitudes(upper, bits)
    lower_own, lower_twin = gather_amplitudes(lower, bits[::-1])

    def blocks_of(partners, *sources):
        amps, where = [], {}
        for j in partners:
            where[j] = []
            for source in sources:
                array, index = source[j]
                if not any(array is other for other in amps):
                    amps.append(array)
                number = [array is other for other in amps].index(True)
                where[j].append((number, index))
        return amps, where

    sums = (rows + 1, CORES * n_rows, tile)
    pairs = (max(cap // 2, 1), 2 * tile, 2 * tile)

    def ladder_call(kernel, found, before, out_shape, extra_scratch, flops, name):
        arrays, layout = [hops[name][hop] for name, hop in found], [groups[name] for name, _ in found]
        partners = sorted({j for part in layout for j in part})
        amps, where = blocks_of(partners, upper_own, lower_own, upper_twin, lower_twin)
        n_units = sum(len(part) for part in layout)
        return pl.pallas_call(
            functools.partial(kernel, cap, layout, where),
            out_shape=out_shape,
            in_specs=[in_vmem] * (len(before) + len(amps) + len(arrays)),
            out_specs=[in_vmem] * len(out_shape),
            scratch_shapes=extra_scratch
            + [
                pltpu.VMEM((n_units, tile), jnp.int32),
                pltpu.SMEM((n_units, tile), jnp.int32),
                pltpu.VMEM(pairs, dtype),
                pltpu.SemaphoreType.DMA,
            ],
            compiler_params=params(
                ((n_units, height, tile), dtype),
                *[(sums, jnp.float32)] * 4,
                ((n_v, CORES * n_rows, width), dtype),
            ),
            cost_estimate=pl.CostEstimate(
                flops=flops,
                bytes_accessed=1024 * 1024,
                transcendentals=0,
            ),
            name=name,
        )(*before, *amps, *arrays)

    virtual = virtual_energy.reshape(1, width)
    whole = jax.ShapeDtypeStruct((n_rows, width), jnp.float32)
    all_sums = jax.ShapeDtypeStruct(sums, jnp.float32)
    total, occupied, inverse = ladder_call(
        first_ladder_kernel,
        [("near", 0), ("early", 0), ("late", 0), ("first", 1), ("late", 1)],
        [occupied_energy.reshape(-1, tile), virtual],
        [all_sums, jax.ShapeDtypeStruct((n_rows, tile), jnp.float32), whole],
        [],
        FIRST_FLOPS,
        "ladder_first",
    )
    for hop in range(2, n_z):
        for name in ("first", "late"):
            hops[name].append(next_on_ring(hops[name][-1], f"{name}_hop_{hop}"))
    total, base = ladder_call(
        middle_ladder_kernel,
        [(name, hop) for hop in range(2, n_z - 1) for name in ("first", "late")],
        [total, driver_terms, amplitudes, occupied, virtual],
        [all_sums, whole],
        [],
        MIDDLE_FLOPS,
        "ladder_middle",
    )
    base, twin = ladder_call(
        last_ladder_kernel,
        [("first", n_z - 1)],
        [total, base],
        [whole, jax.ShapeDtypeStruct((rows, n_rows, tile), jnp.bfloat16)],
        [pltpu.VMEM(sums, jnp.float32)],
        LAST_FLOPS,
        "ladder_last",
    )
    last, behind = after(hops["late"][-1], twin), groups["late"]
    twin = across_core(twin)

    n_last = CORES * len(behind)
    amps, where = blocks_of(behind, upper_own, lower_own)
    sums = (rows + 1, n_rows, tile)
    return pl.pallas_call(
        functools.partial(update_kernel, cap, behind, where),
        out_shape=[
            jax.ShapeDtypeStruct((n_rows, width), jnp.bfloat16),
            jax.ShapeDtypeStruct((n_rows, width), jnp.float32),
        ],
        in_specs=[in_smem] + [in_vmem] * (4 + len(amps) + CORES),
        out_specs=[in_hbm] * 2,
        scratch_shapes=[
            pltpu.VMEM((n_rows, width), jnp.bfloat16),
            pltpu.VMEM((n_rows, width), jnp.float32),
            pltpu.VMEM((n_last, tile), jnp.int32),
            pltpu.SMEM((n_last, tile), jnp.int32),
            pltpu.VMEM(pairs, dtype),
            pltpu.VMEM(sums, jnp.float32),
            pltpu.SemaphoreType.DMA,
            pltpu.SemaphoreType.DMA((2, rows)),
        ],
        compiler_params=params(
            ((n_v, n_rows, width), dtype), ((n_last, height, tile), dtype), *[(sums, jnp.float32)] * 5
        ),
        name="update",
    )(
        tile_live,
        amplitudes,
        base,
        inverse,
        twin,
        *amps,
        last,
        across_core(last),
    )


def solution(mesh):
    in_specs = (
        P("opair", "vpair"),
        P("opair", "vpair"),
        P("vpair", "opair", None, None),
        P("vpair", "opair"),
        P("opair", "vpair"),
        P("opair"),
        P("vpair"),
    )
    out_specs = (P("opair", "vpair"), P("opair", "vpair"))
    return jax.shard_map(
        on_device, mesh=mesh, in_specs=in_specs, out_specs=out_specs, check_vma=False
    )
```
